32 devices in a mesh: space: 8 (over z, x), segment: 4 (over y, core).
Axes of the slice: x: 2, y: 2, z: 4, core: 2. Of those that a mesh axis runs over, the one named last changes fastest.
Arguments:
- field: bfloat16 [4, 64, 8, 8, 128], P(None, 'space'), may hold values from -6 to 6
- depth_kernel: bfloat16 [8, 49, 128], P('segment'), may hold values from -0.875 to 0.875
- depth_bias: bfloat16 [8, 128], P('segment'), may hold values from -3 to 3
- norm_gain: bfloat16 [8, 128], P('segment'), may hold values from 0.099609375 to 1.8984375
- up_weight: bfloat16 [8, 128, 512], P('segment'), may hold values from -0.5 to 0.5
- up_bias: bfloat16 [8, 512], P('segment'), may hold values from -3 to 3
- down_weight: bfloat16 [8, 512, 128], P('segment'), may hold values from -0.25 to 0.25
- scale_exponent: int32 [8, 128], P('segment'), may hold values from -3 to 1
- live_count: int32 [8], P('space'), may hold values from 4 to 8, as said below
- neighbours: int32 [64, 8], P('space'), may hold values from -1 to 63, as said below
- rotations: int32 [64, 8], P('space'), may hold values from 0 to 3
Outputs:
- boundary: bfloat16 [4, 4, 64, 8, 8, 128], P('segment', None, 'space')
The draws below stay inside these ranges and needn't reach their ends.
Inputs may be any that keep to these rules, and one draw needn't show every extreme that they name: `live_count`: at least one index of space holds 8 land patches. `neighbours`: every entry of a live slot is -1, a live slot of the same index of space, one of the first 1 slots of the next index along space, or one of the last 1 slots of the previous one, counted around the cycle; entries of slots that are not live are -1.
All inputs are finite; a program needn't handle non-finite values.
Results may differ from the reference program's by a relative error of at most 0.03.
Values may be sent and summed in bfloat16 or wider, within the bound.
A program may use at most 64 MiB of HBM per device.

```python
import jax
import jax.numpy as jnp
from jax import lax

C = 128
HID = 512
KS = 7
PS = 8
BPS = 2
EDGE = 1
PD = 8
MEMBERS = 4
NPATCH = 64
BLOCKS = 8


def land_counts(key):
    inner = jax.random.fold_in(key, 11)
    first, second = jax.random.split(inner)
    devices = NPATCH // PD
    lowest = max(2 * EDGE, PD // 2)
    counts = jax.random.randint(first, (devices,), lowest, PD + 1)
    fullest = jax.random.randint(second, (), 0, devices)
    return counts.at[fullest].set(PD).astype(jnp.int32)


def draw_live_count(key, part):
    return land_counts(key)


def draw_neighbours(key, part):
    counts = land_counts(key)
    devices = NPATCH // PD
    inner = jax.random.fold_in(key, 23)
    first, second, third, fourth = jax.random.split(inner, 4)
    slots = jnp.arange(NPATCH, dtype=jnp.int32)
    owner = slots // PD
    within = slots % PD
    offset = jax.random.randint(first, (NPATCH, 8), -1, 2)
    target = (owner[:, None] + offset) % devices
    pick = jax.random.randint(second, (NPATCH, 8), 0, 1 << 20)
    own_count = counts[owner][:, None]
    ranked = pick % own_count
    own_pos = jnp.where(ranked < own_count - EDGE, ranked, ranked + PD - own_count)
    edge_pick = jax.random.randint(fourth, (NPATCH, 8), 0, EDGE)
    next_pos = edge_pick
    prev_pos = PD - EDGE + edge_pick
    position = jnp.where(offset == 0, own_pos, jnp.where(offset == 1, next_pos, prev_pos))
    linked = target * PD + position
    ocean = jax.random.randint(third, (NPATCH, 8), 0, 4) == 0
    alive = (within < counts[owner] - EDGE) | (within >= PD - EDGE)
    return jnp.where(ocean | jnp.logical_not(alive)[:, None], -1, linked).astype(jnp.int32)


def place_ends(array, rng, least, largest):
    longest = array.shape.index(max(array.shape))
    spots = []
    for shift in (0, 1):
        where = [jax.random.randint(jax.random.fold_in(rng, axis), (), 0, length) for axis, length in enumerate(array.shape)]
        where[longest] = (where[longest] + shift) % array.shape[longest]
        spots.append(tuple(where))
    return array.at[spots[0]].set(least).at[spots[1]].set(largest)


def steps_of(rng, shape, cuts, low, largest):
    def one(dim, shards_of):
        steps = jax.random.uniform(jax.random.fold_in(jax.random.fold_in(rng, 6), dim), (shards_of,), jnp.float32, low / len(cuts), largest / len(cuts))
        return jnp.repeat(jnp.exp(steps), shape[dim] // shards_of).reshape((-1,) + (1,) * (len(shape) - dim - 1))

    loudness = one(*cuts[0])
    for cut in cuts[1:]:
        loudness = loudness * one(*cut)
    return loudness


def bell_draw(stream_key, shape, deviation, reach, cuts=(), kind=jnp.bfloat16):
    level = steps_of(stream_key, shape, cuts, -0.22, 0.18) if cuts else 1.0
    drawn = jax.random.normal(stream_key, shape, jnp.float32) * deviation * level
    return jnp.minimum(jnp.maximum(drawn, -reach), reach).astype(kind)


def setup_inputs(seed: int = 0) -> dict:
    arg_keys = jax.random.split(jax.random.key(seed), 12)
    return {
        "field": bell_draw(arg_keys[0], (MEMBERS, NPATCH, PS, PS, C), 1.0, 6.0, ((1, 8),)),
        "depth_kernel": bell_draw(arg_keys[1], (BLOCKS, KS * KS, C), (KS * KS) ** -0.5, 0.875, ((0, 4),)),
        "depth_bias": bell_draw(arg_keys[2], (BLOCKS, C), 0.5, 3.0, ((0, 4),)),
        "norm_gain": jnp.clip(1.0 + 0.18 * jax.random.normal(arg_keys[3], (BLOCKS, C), jnp.float32), 0.099609375, 1.8984375).astype(jnp.bfloat16),
        "up_weight": bell_draw(arg_keys[4], (BLOCKS, C, HID), C ** -0.5, 0.5, ((0, 4),)),
        "up_bias": bell_draw(arg_keys[5], (BLOCKS, HID), 0.5, 3.0, ((0, 4),)),
        "down_weight": bell_draw(arg_keys[6], (BLOCKS, HID, C), HID ** -0.5, 0.25, ((0, 4),)),
        "scale_exponent": place_ends(jax.random.randint(arg_keys[7], (BLOCKS, C), -3, 2), jax.random.fold_in(arg_keys[7], 1), -3, 1).astype(jnp.int32),
        "live_count": draw_live_count(jax.random.fold_in(arg_keys[11], 71), 0),
        "neighbours": draw_neighbours(jax.random.fold_in(arg_keys[11], 71), 0),
        "rotations": place_ends(jax.random.randint(arg_keys[10], (NPATCH, 8), 0, 4), jax.random.fold_in(arg_keys[10], 1), 0, 3).astype(jnp.int32),
    }


def rotate_tiles(tiles, turns):
    result = tiles
    for quarter in (1, 2, 3):
        turned = jnp.rot90(tiles, quarter, axes=(2, 3))
        result = jnp.where((turns == quarter)[:, :, None, None, None], turned, result)
    return result

def assemble(tiles, center, margin):
    upper = jnp.concatenate([tiles[:, 0, -margin:, -margin:], tiles[:, 1, -margin:, :], tiles[:, 2, -margin:, :margin]], axis=2)
    middle = jnp.concatenate([tiles[:, 3, :, -margin:], center, tiles[:, 4, :, :margin]], axis=2)
    lower = jnp.concatenate([tiles[:, 5, :margin, -margin:], tiles[:, 6, :margin, :], tiles[:, 7, :margin, :margin]], axis=2)
    return jnp.concatenate([upper, middle, lower], axis=1)

def apply_block(state, tiles, live, kernel, kernel_bias, gain, weight_up, bias_up, weight_down, gamma):
    margin = KS // 2
    side = state.shape[1]
    chans = state.shape[3]
    extended = assemble(tiles, state, margin)
    total = jnp.zeros(state.shape, jnp.float32) + kernel_bias.astype(jnp.float32)
    for row in range(KS):
        for column in range(KS):
            window = extended[:, row:row + side, column:column + side, :].astype(jnp.float32)
            total = total + window * kernel[row * KS + column].astype(jnp.float32)
    mean = lax.optimization_barrier(jnp.mean(total, axis=-1, keepdims=True))
    centred = total - mean
    variance = lax.optimization_barrier(jnp.mean(centred * centred, axis=-1, keepdims=True))
    normed = (centred * lax.rsqrt(variance + 1e-06) * gain.astype(jnp.float32)).astype(jnp.bfloat16)
    flat = normed.reshape(-1, chans)
    hidden = jax.nn.gelu(jnp.dot(flat, weight_up, preferred_element_type=jnp.float32) + bias_up.astype(jnp.float32), approximate=False).astype(jnp.bfloat16)
    branch = jnp.dot(hidden, weight_down, preferred_element_type=jnp.float32).reshape(state.shape)
    return ((state.astype(jnp.float32) + gamma * branch) * live[:, None, None, None]).astype(jnp.bfloat16)

def reference(field, depth_kernel, depth_bias, norm_gain, up_weight, up_bias, down_weight, scale_exponent, live_count, neighbours, rotations):
    slots = jnp.arange(NPATCH, dtype=jnp.int32)
    within = slots % PD
    owned = live_count[slots // PD]
    live = ((within < owned - EDGE) | (within >= PD - EDGE)).astype(jnp.float32)
    gamma = jnp.exp2(scale_exponent.astype(jnp.float32) * 0.5)
    links = jnp.where(neighbours < 0, NPATCH, neighbours).astype(jnp.int32)
    sections = []
    for member in range(MEMBERS):
        state = field[member]
        results = []
        for block in range(BLOCKS):
            padded = jnp.concatenate([state, jnp.zeros((1,) + state.shape[1:], state.dtype)], axis=0)
            tiles = rotate_tiles(padded[links], rotations)
            state = apply_block(state, tiles, live, depth_kernel[block], depth_bias[block], norm_gain[block], up_weight[block], up_bias[block], down_weight[block], gamma[block])
            if (block + 1) % BPS == 0:
                results.append(state)
        sections.append(jnp.stack(results, axis=0))
    return jnp.stack(sections, axis=1)
```

```python
import functools

import jax
import jax.numpy as jnp
import numpy as np
from jax import lax
from jax.experimental import pallas as pl
from jax.experimental.pallas import tpu as pltpu
from jax.sharding import PartitionSpec as P

KS = 7
BPS = 2
EDGE = 1
MARGIN = KS // 2
PS = 8
CELLS = PS * PS
EXT = PS + 2 * MARGIN
WIDE = 3 * PS
ROWS = EXT * WIDE
TURNS = 4
MESH = pl.DeviceIdType.MESH
HOLDERS = {8: (0, 1, 2, 3, 5, 7, 6, 4)}

BIAS = KS * KS
GAIN = BIAS + 1
SCALE = GAIN + 1
UP_BIAS = SCALE + 1


def bases(neighbours, rotations, place, devices, tiles):
    count = neighbours.shape[0]
    local = neighbours - place * count
    following = lax.rem(place + 1, devices) * count
    slot = jnp.where(neighbours == following, count + 1, count)
    slot = jnp.where(jnp.logical_and(local >= 0, local < count), local, slot)
    slot = jnp.where(neighbours < 0, count + 2, slot)
    return (rotations * tiles + slot) * PS


def lookup(table, index):
    value = index
    for k, entry in enumerate(table):
        if entry != k:
            value = jnp.where(index == k, entry, value)
    return value


def position(space, devices):
    return lookup([HOLDERS.get(devices, range(devices)).index(k) for k in range(devices)], space)


def holder(place, devices):
    return lookup(HOLDERS.get(devices, range(devices)), place)


def gelu2(x):
    return x * (1.0 + lax.erf(x * np.float32(0.5**0.5)))


def kernel(
    segments,
    devices,
    blocks,
    field,
    taps,
    bias,
    gain,
    up,
    up_bias,
    down,
    scale,
    live_count,
    neighbours,
    rotations,
    out,
    v_taps,
    v_bias,
    v_gain,
    v_up_bias,
    v_scale,
    v_neighbours,
    v_rotations,
    meta,
    here,
    links,
    win,
    edges,
    ups,
    downs,
    small,
    tiles_a,
    tiles_b,
    ext,
    loc_sem,
    own_sem,
    w_recv,
    fwd_sem,
    h_send,
    h_recv,
    f_send,
    f_recv,
    o_send,
    o_recv,
    in_sem,
):
    space = lax.axis_index("space")
    me = lax.axis_index("segment")
    rows = win.shape[1]
    count = rows // CELLS
    tiles = count + 3
    place = position(space, devices)
    following = lax.rem(place + 1, devices)
    preceding = lax.rem(place + devices - 1, devices)
    after = holder(following, devices)
    before = holder(preceding, devices)
    core = lax.rem(me, 2)
    pair = me // 2
    partner = pair * 2 + (1 - core)
    pairs = segments // 2
    mine = me * BPS

    own_up = pltpu.make_async_copy(up, ups.at[pl.ds(mine, BPS)], loc_sem.at[0])
    own_up.start()
    own_down = pltpu.make_async_copy(down, downs.at[pl.ds(mine, BPS)], loc_sem.at[1])
    own_down.start()
    loads = [
        pltpu.make_async_copy(src, dst, in_sem.at[n])
        for n, (src, dst) in enumerate(
            (
                (neighbours, v_neighbours),
                (rotations, v_rotations),
                (taps, v_taps),
                (bias, v_bias),
                (gain, v_gain),
                (up_bias, v_up_bias),
                (scale, v_scale),
            )
        )
    ]
    for load in loads:
        load.start()
    order = [count - 1, *range(count - 1)]
    half = 2 + (count - 2) // 2
    hid = up_bias.shape[1]
    chans = up.shape[1]
    barrier = pltpu.get_barrier_semaphore()
    new_home = holder(space, devices)

    def greet(where, segment):
        other = jnp.logical_or(where != space, segment != me)

        @pl.when(other)
        def _():
            pl.semaphore_signal(
                barrier, inc=1, device_id=(where, segment), device_id_type=MESH
            )

        return jnp.where(other, 1, 0)

    greetings = 0
    for where in (before, after, preceding, place, following):
        greetings += greet(where, me)
    for step in range(1, segments):
        greetings += greet(space, lax.rem(me + step, segments))
    for segment in range(segments):
        greetings += greet(new_home, segment)

    for load in loads:
        load.wait()
    meta[...] = jnp.full(meta.shape, live_count[0], jnp.int32)
    meta[0:count, 0:8] = bases(v_neighbours[...], v_rotations[...], space, devices, tiles)
    for k in range(BPS):
        small[mine + k, 0 : KS * KS, :] = v_taps[:, k, :].astype(jnp.float32)
        small[mine + k, BIAS : BIAS + 1, :] = v_bias[k : k + 1, :].astype(jnp.float32)
        small[mine + k, GAIN : GAIN + 1, :] = v_gain[k : k + 1, :].astype(jnp.float32)
        small[mine + k, SCALE : SCALE + 1, :] = 0.5 * jnp.exp2(
            v_scale[k : k + 1, :].astype(jnp.float32) * 0.5
        )
        for q in range(hid // chans):
            small[mine + k, UP_BIAS + q : UP_BIAS + q + 1, :] = v_up_bias[
                k : k + 1, q * chans : (q + 1) * chans
            ].astype(jnp.float32)
    def flat(ref):
        return ref.reshape(ref.shape[0] * PS, chans)

    empty = jnp.zeros((CELLS, chans), jnp.float32)
    for turn in range(TURNS):
        at = (turn * tiles + count + 2) * CELLS
        flat(tiles_a)[at : at + CELLS, :] = empty
        flat(tiles_b)[at : at + CELLS, :] = empty
    pl.semaphore_wait(barrier, greetings)

    def send(src, dst, where, segment, send_sem, recv_sem):
        same = jnp.logical_and(where == space, segment == me)

        @pl.when(same)
        def _():
            pltpu.make_async_copy(src, dst, recv_sem).start()

        @pl.when(jnp.logical_not(same))
        def _():
            pltpu.make_async_remote_copy(
                src_ref=src,
                dst_ref=dst,
                send_sem=send_sem,
                recv_sem=recv_sem,
                device_id=(where, segment),
                device_id_type=MESH,
            ).start()

    def sent(src, dst, where, segment, send_sem, recv_sem):
        @pl.when(jnp.logical_not(jnp.logical_and(where == space, segment == me)))
        def _():
            pltpu.make_async_remote_copy(
                src_ref=src,
                dst_ref=dst,
                send_sem=send_sem,
                recv_sem=recv_sem,
                device_id=(where, segment),
                device_id_type=MESH,
            ).wait_send()

    def received(ref, recv_sem):
        pltpu.make_async_copy(ref, ref, recv_sem).wait()

    first = pl.ds(0, CELLS)
    last = pl.ds(rows - CELLS, CELLS)

    def lower(b):
        return edges.at[b, pl.ds(0, CELLS)]

    def upper(b):
        return edges.at[b, pl.ds(CELLS, CELLS)]

    ahead = holder(lax.rem(space + 1, devices), devices)
    behind = holder(lax.rem(space + devices - 1, devices), devices)
    moves = (
        (meta, here, new_home, me, f_send.at[0], f_recv.at[0]),
        (field.at[me, last], lower(0), ahead, me, f_send.at[1], h_recv.at[0, 0]),
        (field.at[me, first], upper(0), behind, me, f_send.at[2], h_recv.at[0, 1]),
        (field.at[me], win.at[0], new_home, me, f_send.at[3], f_recv.at[1]),
    )

    def halo(b, side):
        if side == 0:
            src, dst, to = win.at[b, last], lower(b), after
        else:
            src, dst, to = win.at[b, first], upper(b), before
        return pltpu.make_async_remote_copy(
            src_ref=src,
            dst_ref=dst,
            send_sem=h_send.at[b, side],
            recv_sem=h_recv.at[b, side],
            device_id=(to, me),
            device_id_type=MESH,
        )

    def piece(kind, b, to, send_sem):
        ref = (small, ups, downs)[kind].at[b]
        return pltpu.make_async_remote_copy(
            src_ref=ref,
            dst_ref=ref,
            send_sem=send_sem,
            recv_sem=w_recv.at[kind, b],
            device_id=(space, to),
            device_id_type=MESH,
        )

    def to_partner():
        return [
            piece(kind, mine + k, partner, own_sem.at[k, kind])
            for k in range(BPS)
            for kind in range(3)
        ]

    def to_pairs(k):
        copies = []
        for step in range(1, pairs):
            other = lax.rem(pair + step, pairs) * 2
            at = 3 + (step - 1) * 4
            copies.append(piece(0, mine + k, other, own_sem.at[k, at]))
            copies.append(piece(0, mine + k, other + 1, own_sem.at[k, at + 1]))
            copies.append(piece(1, mine + k, other, own_sem.at[k, at + 2]))
            copies.append(piece(2, mine + k, other + 1, own_sem.at[k, at + 3]))
        return copies

    def forwarded(b, act):
        foreign = b // (2 * BPS) != pair

        @pl.when(jnp.logical_and(foreign, core == 0))
        def _():
            act(piece(1, b, partner, fwd_sem.at[b]))

        @pl.when(jnp.logical_and(foreign, core == 1))
        def _():
            act(piece(2, b, partner, fwd_sem.at[b]))

    def forward(b):
        def act(copy):
            copy.wait_recv()
            copy.start()

        forwarded(b, act)

    def arrive(b):
        owner = b // BPS
        foreign = b // (2 * BPS) != pair

        @pl.when(owner != me)
        def _():
            piece(0, b, partner, fwd_sem.at[b]).wait_recv()

        @pl.when(owner == partner)
        def _():
            piece(1, b, partner, fwd_sem.at[b]).wait_recv()
            piece(2, b, partner, fwd_sem.at[b]).wait_recv()

        @pl.when(jnp.logical_and(foreign, core == 0))
        def _():
            piece(2, b, partner, fwd_sem.at[b]).wait_recv()

        @pl.when(jnp.logical_and(foreign, core == 1))
        def _():
            piece(1, b, partner, fwd_sem.at[b]).wait_recv()

    def outcome(s):
        return (
            win.at[BPS * (s + 1)],
            out.at[me],
            place,
            s,
            o_send.at[s],
            o_recv.at[me],
        )

    def spread(dst, slot, cells):
        dst = flat(dst)
        at = [(turn * tiles + slot) * CELLS for turn in range(TURNS)]
        for i in range(PS):
            row = cells[i * PS : (i + 1) * PS]
            dst[at[0] + i * PS : at[0] + (i + 1) * PS, :] = row
            dst[pl.ds(at[3] + PS - 1 - i, PS, stride=PS), :] = row
        for old, new in ((0, 1), (1, 2)):
            for j in range(PS):
                to = at[new] + (PS - 1 - j) * PS
                dst[to : to + PS, :] = dst[pl.ds(at[old] + j, PS, stride=PS), :]

    def centre(g, i):
        at = g * ROWS + (i + MARGIN) * WIDE + PS
        return slice(at, at + PS)

    def enter(dst, g, cells):
        spread(dst, g, cells)
        for i in range(PS):
            ext[centre(g, i), :] = cells[i * PS : (i + 1) * PS]

    def margins(src, g):
        for d in range(8):
            band_i, band_j = ((0, 0), (0, 1), (0, 2), (1, 0), (1, 2), (2, 0), (2, 1), (2, 2))[d]
            base = links[g, d]
            if band_i == 0:
                lines = [(PS - MARGIN + i, i) for i in range(MARGIN)]
            elif band_i == 1:
                lines = [(i, MARGIN + i) for i in range(PS)]
            else:
                lines = [(i, MARGIN + PS + i) for i in range(MARGIN)]
            for i, to in lines:
                at = g * ROWS + to * WIDE + band_j * PS
                ext[at : at + PS, :] = src[base + i]

    def convolve(b, g):
        total = jnp.broadcast_to(small[b, BIAS : BIAS + 1, :][None], (PS, PS, chans))
        for e in range(KS):
            base = g * ROWS + PS - MARGIN + e
            column = jnp.concatenate(
                [ext[base + i * WIDE : base + i * WIDE + PS, :][None] for i in range(EXT)], axis=0
            )
            for a in range(KS):
                tap = small[b, a * KS + e : a * KS + e + 1, :][None]
                total = total + column[a : a + PS] * tap
        total = total.reshape(CELLS, chans)
        centred = total - jnp.mean(total, axis=-1, keepdims=True)
        variance = jnp.mean(centred * centred, axis=-1, keepdims=True)
        scaled = centred * lax.rsqrt(variance + 1e-06) * small[b, GAIN : GAIN + 1, :]
        return scaled.astype(jnp.bfloat16)

    def group(b, begin, end, dst):
        normed = jnp.concatenate([convolve(b, order[n]) for n in range(begin, end)], axis=0)
        wide = jnp.concatenate(
            [small[b, UP_BIAS + q : UP_BIAS + q + 1, :] for q in range(hid // chans)], axis=1
        )
        hidden = jnp.dot(normed, ups[b], preferred_element_type=jnp.float32) + wide
        hidden = gelu2(hidden).astype(jnp.bfloat16)
        branch = jnp.dot(hidden, downs[b], preferred_element_type=jnp.float32)
        branch = branch * small[b, SCALE : SCALE + 1, :]
        for n in range(begin, end):
            g = order[n]
            alive = jnp.logical_or(g < links[count, 0] - EDGE, g >= count - EDGE)
            alive = jnp.where(alive, 1.0, 0.0)
            old = jnp.concatenate([ext[centre(g, i), :] for i in range(PS)], axis=0)
            state = old + branch[(n - begin) * CELLS : (n - begin + 1) * CELLS]
            state = (state * alive).astype(jnp.bfloat16)
            win[b + 1, g * CELLS : (g + 1) * CELLS, :] = state
            enter(dst, g, state.astype(jnp.float32))

    for move in moves:
        send(*move)
    own_up.wait()
    own_down.wait()

    @pl.when(core == 0)
    def _():
        for copy in to_pairs(0):
            copy.start()

    for copy in to_partner():
        copy.start()
    forward(0)
    received(here, f_recv.at[0])
    table = pltpu.make_async_copy(here, links, loc_sem.at[2])
    table.start()
    received(win.at[0], f_recv.at[1])
    for g in range(count):
        enter(tiles_a, g, win[0, g * CELLS : (g + 1) * CELLS, :].astype(jnp.float32))
    table.wait()

    def layer(s, part):
        b = s * BPS + part
        src, dst = (tiles_a, tiles_b) if part % 2 == 0 else (tiles_b, tiles_a)
        arrive(b)
        for k in range(BPS):
            for c in range(2):
                if k + c and (k + 2 * c - 1) % BPS == part:

                    @pl.when(jnp.logical_and(b == k + 2 * c - 1, core == c))
                    def _():
                        for copy in to_pairs(k):
                            copy.start()

        received(lower(b), h_recv.at[b, 0])
        received(upper(b), h_recv.at[b, 1])
        for side in range(2):
            tile = edges[b, side * CELLS : (side + 1) * CELLS, :].astype(jnp.float32)
            spread(src, count + side, tile)
        for n in range(2):
            margins(src, order[n])
        group(b, 0, 2, dst)

        @pl.when(b < blocks - 1)
        def _():
            halo(b + 1, 0).start()
            halo(b + 1, 1).start()

        for n in range(2, count):
            margins(src, order[n])
        group(b, 2, half, dst)
        group(b, half, count, dst)

        @pl.when(b < blocks - 1)
        def _():
            forward(b + 1)

    def section(s, carry):
        for part in range(BPS):
            layer(s, part)
        send(*outcome(s))
        return carry

    lax.fori_loop(0, segments, section, 0)

    for copy in to_partner() + [copy for k in range(BPS) for copy in to_pairs(k)]:
        copy.wait_send()
    for move in moves:
        sent(*move)

    def drain(b, carry):
        @pl.when(b > 0)
        def _():
            halo(b, 0).wait_send()
            halo(b, 1).wait_send()

        forwarded(b, lambda copy: copy.wait_send())
        return carry

    lax.fori_loop(0, blocks, drain, 0)
    for s in range(segments):
        sent(*outcome(s))
    for member in range(segments):
        received(out.at[member], o_recv.at[member])


def body(
    field,
    depth_kernel,
    depth_bias,
    norm_gain,
    up_weight,
    up_bias,
    down_weight,
    scale_exponent,
    live_count,
    neighbours,
    rotations,
):
    members, count = field.shape[:2]
    chans = field.shape[-1]
    hid = up_weight.shape[-1]
    segments = lax.axis_size("segment")
    devices = lax.axis_size("space")
    blocks = segments * BPS
    assert members == segments and segments % 2 == 0 and count % 2 == 0
    assert BPS % 2 == 0 and devices % 2 == 0
    pairs = segments // 2
    metas = count + 8
    smalls = -(-(UP_BIAS + hid // chans) // 8) * 8
    smem = pl.BlockSpec(memory_space=pltpu.SMEM)
    hbm = pl.BlockSpec(memory_space=pl.ANY)
    dma = pltpu.SemaphoreType.DMA
    out = pl.pallas_call(
        functools.partial(kernel, segments, devices, blocks),
        out_shape=jax.ShapeDtypeStruct((members, count * CELLS, chans), jnp.bfloat16),
        in_specs=[hbm] * 8 + [smem] + [hbm] * 2,
        out_specs=pl.BlockSpec(memory_space=pl.ANY),
        scratch_shapes=[
            pltpu.VMEM((KS * KS, BPS, chans), jnp.bfloat16),
            pltpu.VMEM((BPS, chans), jnp.bfloat16),
            pltpu.VMEM((BPS, chans), jnp.bfloat16),
            pltpu.VMEM((BPS, hid), jnp.bfloat16),
            pltpu.VMEM((BPS, chans), jnp.int32),
            pltpu.VMEM(neighbours.shape, jnp.int32),
            pltpu.VMEM(rotations.shape, jnp.int32),
            pltpu.VMEM((metas, chans), jnp.int32),
            pltpu.VMEM((metas, chans), jnp.int32),
            pltpu.SMEM((metas, chans), jnp.int32),
            pltpu.VMEM((blocks + 1, count * CELLS, chans), jnp.bfloat16),
            pltpu.VMEM((blocks, 2 * CELLS, chans), jnp.bfloat16),
            pltpu.VMEM((blocks, chans, hid), jnp.bfloat16),
            pltpu.VMEM((blocks, hid, chans), jnp.bfloat16),
            pltpu.VMEM((blocks, smalls, chans), jnp.float32),
            pltpu.VMEM((TURNS * (count + 3) * PS, PS, chans), jnp.float32),
            pltpu.VMEM((TURNS * (count + 3) * PS, PS, chans), jnp.float32),
            pltpu.VMEM((count * ROWS, chans), jnp.float32),
            dma((3,)),
            dma((BPS, 3 + 4 * (pairs - 1))),
            dma((3, blocks)),
            dma((blocks,)),
            dma((blocks, 2)),
            dma((blocks, 2)),
            dma((4,)),
            dma((2,)),
            dma((segments,)),
            dma((members,)),
            dma((7,)),
        ],
        compiler_params=pltpu.CompilerParams(
            collective_id=0, has_side_effects=True, vmem_limit_bytes=60 * 2**20
        ),
    )(
        field.reshape(members, count * CELLS, chans),
        jnp.transpose(depth_kernel, (1, 0, 2)),
        depth_bias,
        norm_gain,
        up_weight,
        up_bias,
        down_weight,
        scale_exponent,
        live_count,
        neighbours,
        rotations,
    )
    return out.reshape((1,) + field.shape)


def solution(mesh):
    in_specs = (
        P(None, "space", None, None, None),
        P("segment", None, None),
        P("segment", None),
        P("segment", None),
        P("segment", None, None),
        P("segment", None),
        P("segment", None, None),
        P("segment", None),
        P("space"),
        P("space", None),
        P("space", None),
    )
    out_specs = P("segment", None, "space", None, None, None)
    return jax.shard_map(body, mesh=mesh, in_specs=in_specs, out_specs=out_specs, check_vma=False)
```

```python
import functools

import jax
import jax.numpy as jnp
import numpy as np
from jax import lax
from jax.experimental import pallas as pl
from jax.experimental.pallas import tpu as pltpu
from jax.sharding import PartitionSpec as P

KS = 7
BPS = 2
EDGE = 1
MARGIN = KS // 2
PS = 8
CELLS = PS * PS
EXT = PS + 2 * MARGIN
WIDE = 3 * PS
TURNS = 4
MESH = pl.DeviceIdType.MESH
HOLDERS = {8: (0, 1, 2, 3, 5, 7, 6, 4)}

BIAS = 0
GAIN = 1
SCALE = 2
UP_BIAS = 3


def bases(neighbours, rotations, place, devices, tiles):
    count = neighbours.shape[0]
    local = neighbours - place * count
    following = lax.rem(place + 1, devices) * count
    slot = jnp.where(neighbours == following, count + 1, count)
    slot = jnp.where(jnp.logical_and(local >= 0, local < count), local, slot)
    slot = jnp.where(neighbours < 0, count + 2, slot)
    return (rotations * tiles + slot) * PS


def lookup(table, index):
    value = index
    for k, entry in enumerate(table):
        if entry != k:
            value = jnp.where(index == k, entry, value)
    return value


def position(space, devices):
    return lookup([HOLDERS.get(devices, range(devices)).index(k) for k in range(devices)], space)


def holder(place, devices):
    return lookup(HOLDERS.get(devices, range(devices)), place)


def gelu2(x):
    return x * (1.0 + lax.erf(x * np.float32(0.5**0.5)))


def kernel(
    segments,
    devices,
    blocks,
    field,
    taps,
    bias,
    gain,
    up,
    up_bias,
    down,
    scale,
    live_count,
    neighbours,
    rotations,
    out,
    v_taps,
    v_bias,
    v_gain,
    v_up_bias,
    v_scale,
    v_neighbours,
    v_rotations,
    meta,
    here,
    links,
    win,
    edges,
    ups,
    downs,
    small,
    tiles_a,
    tiles_b,
    ext,
    loc_sem,
    own_sem,
    w_recv,
    fwd_sem,
    h_send,
    h_recv,
    f_send,
    f_recv,
    o_send,
    o_recv,
    in_sem,
):
    space = lax.axis_index("space")
    me = lax.axis_index("segment")
    rows = win.shape[1]
    count = rows // CELLS
    tiles = count + 3
    place = position(space, devices)
    following = lax.rem(place + 1, devices)
    preceding = lax.rem(place + devices - 1, devices)
    after = holder(following, devices)
    before = holder(preceding, devices)
    core = lax.rem(me, 2)
    pair = me // 2
    partner = pair * 2 + (1 - core)
    pairs = segments // 2
    mine = me * BPS

    barrier = pltpu.get_barrier_semaphore()
    new_home = holder(space, devices)

    def greet(where, segment):
        other = jnp.logical_or(where != space, segment != me)

        @pl.when(other)
        def _():
            pl.semaphore_signal(
                barrier, inc=1, device_id=(where, segment), device_id_type=MESH
            )

        return jnp.where(other, 1, 0)

    greetings = 0
    for where in (before, after, preceding, place, following):
        greetings += greet(where, me)
    for step in range(1, segments):
        greetings += greet(space, lax.rem(me + step, segments))
    for segment in range(segments):
        greetings += greet(new_home, segment)

    own_up = pltpu.make_async_copy(up, ups.at[pl.ds(mine, BPS)], loc_sem.at[0])
    own_up.start()
    own_down = pltpu.make_async_copy(down, downs.at[pl.ds(mine, BPS)], loc_sem.at[1])
    own_down.start()
    loads = [
        pltpu.make_async_copy(src, dst, in_sem.at[n])
        for n, (src, dst) in enumerate(
            (
                (neighbours, v_neighbours),
                (rotations, v_rotations),
                (taps, v_taps),
                (bias, v_bias),
                (gain, v_gain),
                (up_bias, v_up_bias),
                (scale, v_scale),
            )
        )
    ]
    for load in loads:
        load.start()
    order = [count - 1, *range(count - 1)]
    half = 2 + (count - 2) // 2
    hid = up_bias.shape[1]
    chans = up.shape[1]
    for load in loads:
        load.wait()
    meta[...] = jnp.full(meta.shape, live_count[0], jnp.int32)
    meta[0:count, 0:8] = bases(v_neighbours[...], v_rotations[...], space, devices, tiles)
    for k in range(BPS):
        for row in range(KS):
            small[mine + k, row, 0:KS, :] = v_taps[
                row * KS : (row + 1) * KS, k, :
            ].astype(jnp.float32)
        small[mine + k, KS, BIAS : BIAS + 1, :] = v_bias[k : k + 1, :].astype(jnp.float32)
        small[mine + k, KS, GAIN : GAIN + 1, :] = v_gain[k : k + 1, :].astype(jnp.float32)
        small[mine + k, KS, SCALE : SCALE + 1, :] = 0.5 * jnp.exp2(
            v_scale[k : k + 1, :].astype(jnp.float32) * 0.5
        )
        for q in range(hid // chans):
            small[mine + k, KS, UP_BIAS + q : UP_BIAS + q + 1, :] = v_up_bias[
                k : k + 1, q * chans : (q + 1) * chans
            ].astype(jnp.float32)

    def flat(ref):
        return ref.reshape(ref.shape[0] * PS, chans)

    empty = jnp.zeros((CELLS, chans), jnp.float32)
    for turn in range(TURNS):
        at = (turn * tiles + count + 2) * CELLS
        flat(tiles_a)[at : at + CELLS, :] = empty
        flat(tiles_b)[at : at + CELLS, :] = empty
    pl.semaphore_wait(barrier, greetings)

    def send(src, dst, where, segment, send_sem, recv_sem):
        same = jnp.logical_and(where == space, segment == me)

        @pl.when(same)
        def _():
            pltpu.make_async_copy(src, dst, recv_sem).start()

        @pl.when(jnp.logical_not(same))
        def _():
            pltpu.make_async_remote_copy(
                src_ref=src,
                dst_ref=dst,
                send_sem=send_sem,
                recv_sem=recv_sem,
                device_id=(where, segment),
                device_id_type=MESH,
            ).start()

    def sent(src, dst, where, segment, send_sem, recv_sem):
        @pl.when(jnp.logical_not(jnp.logical_and(where == space, segment == me)))
        def _():
            pltpu.make_async_remote_copy(
                src_ref=src,
                dst_ref=dst,
                send_sem=send_sem,
                recv_sem=recv_sem,
                device_id=(where, segment),
                device_id_type=MESH,
            ).wait_send()

    def received(ref, recv_sem):
        pltpu.make_async_copy(ref, ref, recv_sem).wait()

    first = pl.ds(0, CELLS)
    last = pl.ds(rows - CELLS, CELLS)

    def lower(b):
        return edges.at[b, pl.ds(0, CELLS)]

    def upper(b):
        return edges.at[b, pl.ds(CELLS, CELLS)]

    ahead = holder(lax.rem(space + 1, devices), devices)
    behind = holder(lax.rem(space + devices - 1, devices), devices)
    moves = (
        (meta, here, new_home, me, f_send.at[0], f_recv.at[0]),
        (field.at[me, last], lower(0), ahead, me, f_send.at[1], h_recv.at[0, 0]),
        (field.at[me, first], upper(0), behind, me, f_send.at[2], h_recv.at[0, 1]),
        (field.at[me], win.at[0], new_home, me, f_send.at[3], f_recv.at[1]),
    )

    def halo(b, side):
        if side == 0:
            src, dst, to = win.at[b, last], lower(b), after
        else:
            src, dst, to = win.at[b, first], upper(b), before
        return pltpu.make_async_remote_copy(
            src_ref=src,
            dst_ref=dst,
            send_sem=h_send.at[b, side],
            recv_sem=h_recv.at[b, side],
            device_id=(to, me),
            device_id_type=MESH,
        )

    def piece(kind, b, to, send_sem):
        ref = (small, ups, downs)[kind].at[b]
        return pltpu.make_async_remote_copy(
            src_ref=ref,
            dst_ref=ref,
            send_sem=send_sem,
            recv_sem=w_recv.at[kind, b],
            device_id=(space, to),
            device_id_type=MESH,
        )

    def to_partner():
        return [
            piece(kind, mine + k, partner, own_sem.at[k, kind])
            for k in range(BPS)
            for kind in range(3)
        ]

    def to_pairs(k):
        copies = []
        for step in range(1, pairs):
            other = lax.rem(pair + step, pairs) * 2
            at = 3 + (step - 1) * 4
            copies.append(piece(0, mine + k, other, own_sem.at[k, at]))
            copies.append(piece(0, mine + k, other + 1, own_sem.at[k, at + 1]))
            copies.append(piece(1, mine + k, other, own_sem.at[k, at + 2]))
            copies.append(piece(2, mine + k, other + 1, own_sem.at[k, at + 3]))
        return copies

    def forwarded(b, act):
        foreign = b // (2 * BPS) != pair

        @pl.when(jnp.logical_and(foreign, core == 0))
        def _():
            act(piece(1, b, partner, fwd_sem.at[b]))

        @pl.when(jnp.logical_and(foreign, core == 1))
        def _():
            act(piece(2, b, partner, fwd_sem.at[b]))

    def forward(b):
        def act(copy):
            copy.wait_recv()
            copy.start()

        forwarded(b, act)

    def arrive(b):
        owner = b // BPS
        foreign = b // (2 * BPS) != pair

        @pl.when(owner != me)
        def _():
            piece(0, b, partner, fwd_sem.at[b]).wait_recv()

        @pl.when(owner == partner)
        def _():
            piece(1, b, partner, fwd_sem.at[b]).wait_recv()
            piece(2, b, partner, fwd_sem.at[b]).wait_recv()

        @pl.when(jnp.logical_and(foreign, core == 0))
        def _():
            piece(2, b, partner, fwd_sem.at[b]).wait_recv()

        @pl.when(jnp.logical_and(foreign, core == 1))
        def _():
            piece(1, b, partner, fwd_sem.at[b]).wait_recv()

    chunks = ((count - 1, 1), (0, 1), (1, half - 2), (half - 1, count - half))

    def outcome(s, n):
        at = pl.ds(chunks[n][0] * CELLS, chunks[n][1] * CELLS)
        return (
            win.at[BPS * (s + 1), at],
            out.at[me, at],
            place,
            s,
            o_send.at[s, n],
            o_recv.at[me, n],
        )

    def spread(dst, slot, cells):
        dst = flat(dst)
        at = [(turn * tiles + slot) * CELLS for turn in range(TURNS)]
        for i in range(PS):
            row = cells[i * PS : (i + 1) * PS]
            dst[at[0] + i * PS : at[0] + (i + 1) * PS, :] = row
            dst[pl.ds(at[3] + PS - 1 - i, PS, stride=PS), :] = row
        for old, new in ((0, 1), (1, 2)):
            for j in range(PS):
                to = at[new] + (PS - 1 - j) * PS
                dst[to : to + PS, :] = dst[pl.ds(at[old] + j, PS, stride=PS), :]

    def middle(g):
        return (slice(g * EXT + MARGIN, g * EXT + MARGIN + PS), slice(PS, 2 * PS))

    def enter(dst, g, cells):
        spread(dst, g, cells)
        ext[middle(g)] = cells.reshape(PS, PS, chans)

    def margins(src, g):
        for d in range(8):
            band_i, band_j = ((0, 0), (0, 1), (0, 2), (1, 0), (1, 2), (2, 0), (2, 1), (2, 2))[d]
            base = links[g, d]
            if band_i == 0:
                lines = [(PS - MARGIN + i, i) for i in range(MARGIN)]
            elif band_i == 1:
                lines = [(i, MARGIN + i) for i in range(PS)]
            else:
                lines = [(i, MARGIN + PS + i) for i in range(MARGIN)]
            for i, to in lines:
                ext[g * EXT + to, band_j * PS : (band_j + 1) * PS, :] = src[base + i]

    def convolve(b, places):
        def line(a, total):
            for e in range(KS):
                window = jnp.concatenate(
                    [
                        ext[pl.ds(g * EXT + a, PS), PS - MARGIN + e : 2 * PS - MARGIN + e, :]
                        for g in places
                    ],
                    axis=0,
                )
                total = total + window * small[b, a, e : e + 1, :][None]
            return total

        start = small[b, KS, BIAS : BIAS + 1, :][None]
        start = jnp.broadcast_to(start, (len(places) * PS, PS, chans))
        total = lax.fori_loop(0, KS, line, start).reshape(-1, chans)
        centred = total - jnp.mean(total, axis=-1, keepdims=True)
        variance = jnp.mean(centred * centred, axis=-1, keepdims=True)
        scaled = centred * lax.rsqrt(variance + 1e-06) * small[b, KS, GAIN : GAIN + 1, :]
        return scaled.astype(jnp.bfloat16)

    def group(b, begin, end):
        normed = convolve(b, order[begin:end])
        wide = jnp.concatenate(
            [small[b, KS, UP_BIAS + q : UP_BIAS + q + 1, :] for q in range(hid // chans)], axis=1
        )
        hidden = jnp.dot(normed, ups[b], preferred_element_type=jnp.float32) + wide
        hidden = gelu2(hidden).astype(jnp.bfloat16)
        branch = jnp.dot(hidden, downs[b], preferred_element_type=jnp.float32)
        branch = branch * small[b, KS, SCALE : SCALE + 1, :]
        for n in range(begin, end):
            g = order[n]
            alive = jnp.logical_or(g < links[count, 0] - EDGE, g >= count - EDGE)
            alive = jnp.where(alive, 1.0, 0.0)
            old = ext[middle(g)].reshape(CELLS, chans)
            state = old + branch[(n - begin) * CELLS : (n - begin + 1) * CELLS]
            state = (state * alive).astype(jnp.bfloat16)
            win[b + 1, g * CELLS : (g + 1) * CELLS, :] = state

    def settle(b, begin, end, dst):
        for n in range(begin, end):
            g = order[n]
            enter(dst, g, win[b + 1, g * CELLS : (g + 1) * CELLS, :].astype(jnp.float32))

    for move in moves:
        send(*move)
    own_up.wait()
    own_down.wait()

    @pl.when(core == 0)
    def _():
        for copy in to_pairs(0):
            copy.start()

    for copy in to_partner():
        copy.start()
    forward(0)
    received(here, f_recv.at[0])
    table = pltpu.make_async_copy(here, links, loc_sem.at[2])
    table.start()
    received(win.at[0], f_recv.at[1])
    for g in range(count):
        enter(tiles_a, g, win[0, g * CELLS : (g + 1) * CELLS, :].astype(jnp.float32))
    table.wait()

    def layer(s, part):
        b = s * BPS + part
        src, dst = (tiles_a, tiles_b) if part % 2 == 0 else (tiles_b, tiles_a)
        arrive(b)
        for k in range(BPS):
            for c in range(2):
                if k + c and (k + 2 * c - 1) % BPS == part:

                    @pl.when(jnp.logical_and(b == k + 2 * c - 1, core == c))
                    def _():
                        for copy in to_pairs(k):
                            copy.start()

        received(lower(b), h_recv.at[b, 0])
        received(upper(b), h_recv.at[b, 1])
        for side in range(2):
            tile = edges[b, side * CELLS : (side + 1) * CELLS, :].astype(jnp.float32)
            spread(src, count + side, tile)
        for n in range(2):
            margins(src, order[n])
        group(b, 0, 2)

        @pl.when(b < blocks - 1)
        def _():
            halo(b + 1, 0).start()
            halo(b + 1, 1).start()

        ends = part == BPS - 1
        if ends:
            send(*outcome(s, 0))
            send(*outcome(s, 1))
        settle(b, 0, 2, dst)
        for n in range(2, count):
            margins(src, order[n])
        group(b, 2, half)
        if ends:
            send(*outcome(s, 2))
        group(b, half, count)
        if ends:
            send(*outcome(s, 3))
        settle(b, 2, count, dst)

        @pl.when(b < blocks - 1)
        def _():
            forward(b + 1)

    def section(s, carry):
        for part in range(BPS):
            layer(s, part)
        return carry

    lax.fori_loop(0, segments, section, 0)

    for copy in to_partner() + [copy for k in range(BPS) for copy in to_pairs(k)]:
        copy.wait_send()
    for move in moves:
        sent(*move)

    def drain(b, carry):
        @pl.when(b > 0)
        def _():
            halo(b, 0).wait_send()
            halo(b, 1).wait_send()

        forwarded(b, lambda copy: copy.wait_send())
        return carry

    lax.fori_loop(0, blocks, drain, 0)
    for s in range(segments):
        for n in range(len(chunks)):
            sent(*outcome(s, n))
    for member in range(segments):
        for n, (start, size) in enumerate(chunks):
            received(out.at[member, pl.ds(start * CELLS, size * CELLS)], o_recv.at[member, n])


def body(
    field,
    depth_kernel,
    depth_bias,
    norm_gain,
    up_weight,
    up_bias,
    down_weight,
    scale_exponent,
    live_count,
    neighbours,
    rotations,
):
    members, count = field.shape[:2]
    chans = field.shape[-1]
    hid = up_weight.shape[-1]
    segments = lax.axis_size("segment")
    devices = lax.axis_size("space")
    blocks = segments * BPS
    assert members == segments and segments % 2 == 0 and count % 2 == 0
    assert BPS % 2 == 0 and devices % 2 == 0
    pairs = segments // 2
    metas = count + 8
    assert UP_BIAS + hid // chans <= PS
    smem = pl.BlockSpec(memory_space=pltpu.SMEM)
    hbm = pl.BlockSpec(memory_space=pl.ANY)
    dma = pltpu.SemaphoreType.DMA
    out = pl.pallas_call(
        functools.partial(kernel, segments, devices, blocks),
        out_shape=jax.ShapeDtypeStruct((members, count * CELLS, chans), jnp.bfloat16),
        in_specs=[hbm] * 8 + [smem] + [hbm] * 2,
        out_specs=pl.BlockSpec(memory_space=pl.ANY),
        scratch_shapes=[
            pltpu.VMEM((KS * KS, BPS, chans), jnp.bfloat16),
            pltpu.VMEM((BPS, chans), jnp.bfloat16),
            pltpu.VMEM((BPS, chans), jnp.bfloat16),
            pltpu.VMEM((BPS, hid), jnp.bfloat16),
            pltpu.VMEM((BPS, chans), jnp.int32),
            pltpu.VMEM(neighbours.shape, jnp.int32),
            pltpu.VMEM(rotations.shape, jnp.int32),
            pltpu.VMEM((metas, chans), jnp.int32),
            pltpu.VMEM((metas, chans), jnp.int32),
            pltpu.SMEM((metas, chans), jnp.int32),
            pltpu.VMEM((blocks + 1, count * CELLS, chans), jnp.bfloat16),
            pltpu.VMEM((blocks, 2 * CELLS, chans), jnp.bfloat16),
            pltpu.VMEM((blocks, chans, hid), jnp.bfloat16),
            pltpu.VMEM((blocks, hid, chans), jnp.bfloat16),
            pltpu.VMEM((blocks, KS + 1, PS, chans), jnp.float32),
            pltpu.VMEM((TURNS * (count + 3) * PS, PS, chans), jnp.float32),
            pltpu.VMEM((TURNS * (count + 3) * PS, PS, chans), jnp.float32),
            pltpu.VMEM((count * EXT, WIDE, chans), jnp.float32),
            dma((3,)),
            dma((BPS, 3 + 4 * (pairs - 1))),
            dma((3, blocks)),
            dma((blocks,)),
            dma((blocks, 2)),
            dma((blocks, 2)),
            dma((4,)),
            dma((2,)),
            dma((segments, 4)),
            dma((members, 4)),
            dma((7,)),
        ],
        compiler_params=pltpu.CompilerParams(
            collective_id=0, has_side_effects=True, vmem_limit_bytes=60 * 2**20
        ),
    )(
        field.reshape(members, count * CELLS, chans),
        jnp.transpose(depth_kernel, (1, 0, 2)),
        depth_bias,
        norm_gain,
        up_weight,
        up_bias,
        down_weight,
        scale_exponent,
        live_count,
        neighbours,
        rotations,
    )
    return out.reshape((1,) + field.shape)


def solution(mesh):
    in_specs = (
        P(None, "space", None, None, None),
        P("segment", None, None),
        P("segment", None),
        P("segment", None),
        P("segment", None, None),
        P("segment", None),
        P("segment", None, None),
        P("segment", None),
        P("space"),
        P("space", None),
        P("space", None),
    )
    out_specs = P("segment", None, "space", None, None, None)
    return jax.shard_map(body, mesh=mesh, in_specs=in_specs, out_specs=out_specs, check_vma=False)
```

```python
import functools

import jax
import jax.numpy as jnp
import numpy as np
from jax import lax
from jax.experimental import pallas as pl
from jax.experimental.pallas import tpu as pltpu
from jax.sharding import PartitionSpec as P

KS = 7
BPS = 2
EDGE = 1
MARGIN = KS // 2
PS = 8
CELLS = PS * PS
EXT = PS + 2 * MARGIN
WIDE = 3 * PS
TURNS = 4
MESH = pl.DeviceIdType.MESH
HOLDERS = {8: (0, 1, 2, 3, 5, 7, 6, 4)}

BIAS = 0
GAIN = 1
SCALE = 2
UP_BIAS = 3


def bases(neighbours, rotations, place, devices, tiles):
    count = neighbours.shape[0]
    local = neighbours - place * count
    following = lax.rem(place + 1, devices) * count
    slot = jnp.where(neighbours == following, count + 1, count)
    slot = jnp.where(jnp.logical_and(local >= 0, local < count), local, slot)
    slot = jnp.where(neighbours < 0, count + 2, slot)
    return (rotations * tiles + slot) * PS


def lookup(table, index):
    value = index
    for k, entry in enumerate(table):
        if entry != k:
            value = jnp.where(index == k, entry, value)
    return value


def position(space, devices):
    return lookup([HOLDERS.get(devices, range(devices)).index(k) for k in range(devices)], space)


def holder(place, devices):
    return lookup(HOLDERS.get(devices, range(devices)), place)


def gelu2(x):
    return x * (1.0 + lax.erf(x * np.float32(0.5**0.5)))


def kernel(
    segments,
    devices,
    blocks,
    field,
    taps,
    bias,
    gain,
    up,
    up_bias,
    down,
    scale,
    live_count,
    neighbours,
    rotations,
    out,
    v_taps,
    v_bias,
    v_gain,
    v_up_bias,
    v_scale,
    v_neighbours,
    v_rotations,
    meta,
    here,
    links,
    win,
    edges,
    ups,
    downs,
    small,
    tiles_a,
    tiles_b,
    ext,
    loc_sem,
    own_sem,
    w_recv,
    fwd_sem,
    h_send,
    h_recv,
    f_send,
    f_recv,
    o_send,
    o_recv,
    in_sem,
):
    space = lax.axis_index("space")
    me = lax.axis_index("segment")
    rows = win.shape[1]
    count = rows // CELLS
    tiles = count + 3
    place = position(space, devices)
    following = lax.rem(place + 1, devices)
    preceding = lax.rem(place + devices - 1, devices)
    after = holder(following, devices)
    before = holder(preceding, devices)
    core = lax.rem(me, 2)
    pair = me // 2
    partner = pair * 2 + (1 - core)
    pairs = segments // 2
    mine = me * BPS

    barrier = pltpu.get_barrier_semaphore()
    new_home = holder(space, devices)

    def greet(where, segment):
        other = jnp.logical_or(where != space, segment != me)

        @pl.when(other)
        def _():
            pl.semaphore_signal(
                barrier, inc=1, device_id=(where, segment), device_id_type=MESH
            )

        return jnp.where(other, 1, 0)

    greetings = 0
    for where in (before, after, preceding, place, following):
        greetings += greet(where, me)
    for step in range(1, segments):
        greetings += greet(space, lax.rem(me + step, segments))
    for segment in range(segments):
        greetings += greet(new_home, segment)

    own_up = pltpu.make_async_copy(up, ups.at[pl.ds(mine, BPS)], loc_sem.at[0])
    own_up.start()
    own_down = pltpu.make_async_copy(down, downs.at[pl.ds(mine, BPS)], loc_sem.at[1])
    own_down.start()
    loads = [
        pltpu.make_async_copy(src, dst, in_sem.at[n])
        for n, (src, dst) in enumerate(
            (
                (neighbours, v_neighbours),
                (rotations, v_rotations),
                (taps, v_taps),
                (bias, v_bias),
                (gain, v_gain),
                (up_bias, v_up_bias),
                (scale, v_scale),
            )
        )
    ]
    for load in loads:
        load.start()
    order = [count - 1, *range(count - 1)]
    half = 2 + (count - 2) // 2
    hid = up_bias.shape[1]
    chans = up.shape[1]
    for load in loads:
        load.wait()
    meta[...] = jnp.full(meta.shape, live_count[0], jnp.int32)
    meta[0:count, 0:8] = bases(v_neighbours[...], v_rotations[...], space, devices, tiles)
    for k in range(BPS):
        for row in range(KS):
            small[mine + k, row, 0:KS, :] = v_taps[
                row * KS : (row + 1) * KS, k, :
            ].astype(jnp.float32)
        small[mine + k, KS, BIAS : BIAS + 1, :] = v_bias[k : k + 1, :].astype(jnp.float32)
        small[mine + k, KS, GAIN : GAIN + 1, :] = v_gain[k : k + 1, :].astype(jnp.float32)
        small[mine + k, KS, SCALE : SCALE + 1, :] = 0.5 * jnp.exp2(
            v_scale[k : k + 1, :].astype(jnp.float32) * 0.5
        )
        for q in range(hid // chans):
            small[mine + k, KS, UP_BIAS + q : UP_BIAS + q + 1, :] = v_up_bias[
                k : k + 1, q * chans : (q + 1) * chans
            ].astype(jnp.float32)

    def flat(ref):
        return ref.reshape(ref.shape[0] * PS, chans)

    empty = jnp.zeros((CELLS, chans), jnp.float32)
    for turn in range(TURNS):
        at = (turn * tiles + count + 2) * CELLS
        flat(tiles_a)[at : at + CELLS, :] = empty
        flat(tiles_b)[at : at + CELLS, :] = empty
    pl.semaphore_wait(barrier, greetings)

    def send(src, dst, where, segment, send_sem, recv_sem):
        same = jnp.logical_and(where == space, segment == me)

        @pl.when(same)
        def _():
            pltpu.make_async_copy(src, dst, recv_sem).start()

        @pl.when(jnp.logical_not(same))
        def _():
            pltpu.make_async_remote_copy(
                src_ref=src,
                dst_ref=dst,
                send_sem=send_sem,
                recv_sem=recv_sem,
                device_id=(where, segment),
                device_id_type=MESH,
            ).start()

    def sent(src, dst, where, segment, send_sem, recv_sem):
        @pl.when(jnp.logical_not(jnp.logical_and(where == space, segment == me)))
        def _():
            pltpu.make_async_remote_copy(
                src_ref=src,
                dst_ref=dst,
                send_sem=send_sem,
                recv_sem=recv_sem,
                device_id=(where, segment),
                device_id_type=MESH,
            ).wait_send()

    def received(ref, recv_sem):
        pltpu.make_async_copy(ref, ref, recv_sem).wait()

    first = pl.ds(0, CELLS)
    last = pl.ds(rows - CELLS, CELLS)

    def lower(b):
        return edges.at[b, pl.ds(0, CELLS)]

    def upper(b):
        return edges.at[b, pl.ds(CELLS, CELLS)]

    ahead = holder(lax.rem(space + 1, devices), devices)
    behind = holder(lax.rem(space + devices - 1, devices), devices)
    moves = (
        (meta, here, new_home, me, f_send.at[0], f_recv.at[0]),
        (field.at[me, last], lower(0), ahead, me, f_send.at[1], h_recv.at[0, 0]),
        (field.at[me, first], upper(0), behind, me, f_send.at[2], h_recv.at[0, 1]),
        (field.at[me], win.at[0], new_home, me, f_send.at[3], f_recv.at[1]),
    )

    def halo(b, side):
        if side == 0:
            src, dst, to = win.at[b, last], lower(b), after
        else:
            src, dst, to = win.at[b, first], upper(b), before
        return pltpu.make_async_remote_copy(
            src_ref=src,
            dst_ref=dst,
            send_sem=h_send.at[b, side],
            recv_sem=h_recv.at[b, side],
            device_id=(to, me),
            device_id_type=MESH,
        )

    def piece(kind, b, to, send_sem):
        ref = (small, ups, downs)[kind].at[b]
        return pltpu.make_async_remote_copy(
            src_ref=ref,
            dst_ref=ref,
            send_sem=send_sem,
            recv_sem=w_recv.at[kind, b],
            device_id=(space, to),
            device_id_type=MESH,
        )

    def to_partner():
        return [
            piece(kind, mine + k, partner, own_sem.at[k, kind])
            for k in range(BPS)
            for kind in range(3)
        ]

    def to_pairs(k):
        copies = []
        for step in range(1, pairs):
            other = lax.rem(pair + step, pairs) * 2
            at = 3 + (step - 1) * 4
            copies.append(piece(0, mine + k, other, own_sem.at[k, at]))
            copies.append(piece(0, mine + k, other + 1, own_sem.at[k, at + 1]))
            copies.append(piece(1, mine + k, other, own_sem.at[k, at + 2]))
            copies.append(piece(2, mine + k, other + 1, own_sem.at[k, at + 3]))
        return copies

    def forwarded(b, act):
        foreign = b // (2 * BPS) != pair

        @pl.when(jnp.logical_and(foreign, core == 0))
        def _():
            act(piece(1, b, partner, fwd_sem.at[b]))

        @pl.when(jnp.logical_and(foreign, core == 1))
        def _():
            act(piece(2, b, partner, fwd_sem.at[b]))

    def forward(b):
        def act(copy):
            copy.wait_recv()
            copy.start()

        forwarded(b, act)

    def arrive(b):
        owner = b // BPS
        foreign = b // (2 * BPS) != pair

        @pl.when(owner != me)
        def _():
            piece(0, b, partner, fwd_sem.at[b]).wait_recv()

        @pl.when(owner == partner)
        def _():
            piece(1, b, partner, fwd_sem.at[b]).wait_recv()
            piece(2, b, partner, fwd_sem.at[b]).wait_recv()

        @pl.when(jnp.logical_and(foreign, core == 0))
        def _():
            piece(2, b, partner, fwd_sem.at[b]).wait_recv()

        @pl.when(jnp.logical_and(foreign, core == 1))
        def _():
            piece(1, b, partner, fwd_sem.at[b]).wait_recv()

    chunks = ((count - 1, 1), (0, 1), (1, half - 2), (half - 1, count - half))

    def outcome(s, n):
        at = pl.ds(chunks[n][0] * CELLS, chunks[n][1] * CELLS)
        return (
            win.at[BPS * (s + 1), at],
            out.at[me, at],
            place,
            s,
            o_send.at[s, n],
            o_recv.at[me, n],
        )

    def spread(dst, slot, cells):
        dst = flat(dst)
        at = [(turn * tiles + slot) * CELLS for turn in range(TURNS)]
        for i in range(PS):
            row = cells[i * PS : (i + 1) * PS]
            dst[at[0] + i * PS : at[0] + (i + 1) * PS, :] = row
            dst[pl.ds(at[3] + PS - 1 - i, PS, stride=PS), :] = row
        for old, new in ((0, 1), (1, 2)):
            for j in range(PS):
                to = at[new] + (PS - 1 - j) * PS
                dst[to : to + PS, :] = dst[pl.ds(at[old] + j, PS, stride=PS), :]

    def middle(g):
        return (slice(g * EXT + MARGIN, g * EXT + MARGIN + PS), slice(PS, 2 * PS))

    def enter(dst, g, cells):
        spread(dst, g, cells)
        ext[middle(g)] = cells.reshape(PS, PS, chans)

    def margins(src, g):
        for d in range(8):
            band_i, band_j = ((0, 0), (0, 1), (0, 2), (1, 0), (1, 2), (2, 0), (2, 1), (2, 2))[d]
            base = links[g, d]
            if band_i == 0:
                lines = [(PS - MARGIN + i, i) for i in range(MARGIN)]
            elif band_i == 1:
                lines = [(i, MARGIN + i) for i in range(PS)]
            else:
                lines = [(i, MARGIN + PS + i) for i in range(MARGIN)]
            for i, to in lines:
                ext[g * EXT + to, band_j * PS : (band_j + 1) * PS, :] = src[base + i]

    def convolve(b, places):
        def line(a, total):
            for e in range(KS):
                window = jnp.concatenate(
                    [
                        ext[pl.ds(g * EXT + a, PS), PS - MARGIN + e : 2 * PS - MARGIN + e, :]
                        for g in places
                    ],
                    axis=0,
                )
                total = total + window * small[b, a, e : e + 1, :][None]
            return total

        start = small[b, KS, BIAS : BIAS + 1, :][None]
        start = jnp.broadcast_to(start, (len(places) * PS, PS, chans))
        total = lax.fori_loop(0, KS, line, start).reshape(-1, chans)
        centred = total - jnp.mean(total, axis=-1, keepdims=True)
        variance = jnp.mean(centred * centred, axis=-1, keepdims=True)
        scaled = centred * lax.rsqrt(variance + 1e-06) * small[b, KS, GAIN : GAIN + 1, :]
        return scaled.astype(jnp.bfloat16)

    def group(b, begin, end):
        normed = convolve(b, order[begin:end])
        wide = jnp.concatenate(
            [small[b, KS, UP_BIAS + q : UP_BIAS + q + 1, :] for q in range(hid // chans)], axis=1
        )
        hidden = jnp.dot(normed, ups[b], preferred_element_type=jnp.float32) + wide
        hidden = gelu2(hidden).astype(jnp.bfloat16)
        branch = jnp.dot(hidden, downs[b], preferred_element_type=jnp.float32)
        branch = branch * small[b, KS, SCALE : SCALE + 1, :]
        for n in range(begin, end):
            g = order[n]
            alive = jnp.logical_or(g < links[count, 0] - EDGE, g >= count - EDGE)
            alive = jnp.where(alive, 1.0, 0.0)
            old = ext[middle(g)].reshape(CELLS, chans)
            state = old + branch[(n - begin) * CELLS : (n - begin + 1) * CELLS]
            state = (state * alive).astype(jnp.bfloat16)
            win[b + 1, g * CELLS : (g + 1) * CELLS, :] = state

    def settle(b, begin, end, dst):
        for n in range(begin, end):
            g = order[n]
            enter(dst, g, win[b + 1, g * CELLS : (g + 1) * CELLS, :].astype(jnp.float32))

    for move in moves:
        send(*move)
    own_up.wait()
    own_down.wait()

    @pl.when(core == 0)
    def _():
        for copy in to_pairs(0):
            copy.start()

    for copy in to_partner():
        copy.start()
    forward(0)
    received(here, f_recv.at[0])
    table = pltpu.make_async_copy(here, links, loc_sem.at[2])
    table.start()
    received(win.at[0], f_recv.at[1])
    for g in range(count):
        enter(tiles_a, g, win[0, g * CELLS : (g + 1) * CELLS, :].astype(jnp.float32))
    table.wait()

    def layer(s, part):
        b = s * BPS + part
        src, dst = (tiles_a, tiles_b) if part % 2 == 0 else (tiles_b, tiles_a)
        arrive(b)
        for k in range(BPS):
            for c in range(2):
                if k + c and (k + 2 * c - 1) % BPS == part:

                    @pl.when(jnp.logical_and(b == k + 2 * c - 1, core == c))
                    def _():
                        for copy in to_pairs(k):
                            copy.start()

        received(lower(b), h_recv.at[b, 0])
        received(upper(b), h_recv.at[b, 1])
        for side in range(2):
            tile = edges[b, side * CELLS : (side + 1) * CELLS, :].astype(jnp.float32)
            spread(src, count + side, tile)
        for n in range(2):
            margins(src, order[n])
        group(b, 0, 2)

        @pl.when(b < blocks - 1)
        def _():
            halo(b + 1, 0).start()
            halo(b + 1, 1).start()

        ends = part == BPS - 1
        if ends:
            send(*outcome(s, 0))
            send(*outcome(s, 1))
        settle(b, 0, 2, dst)
        for n in range(2, count):
            margins(src, order[n])
        group(b, 2, half)
        if ends:
            send(*outcome(s, 2))
        group(b, half, count)
        if ends:
            send(*outcome(s, 3))
        settle(b, 2, count, dst)

        @pl.when(b < blocks - 1)
        def _():
            forward(b + 1)

    def section(s, carry):
        for part in range(BPS):
            layer(s, part)
        return carry

    lax.fori_loop(0, segments, section, 0)

    for copy in to_partner() + [copy for k in range(BPS) for copy in to_pairs(k)]:
        copy.wait_send()
    for move in moves:
        sent(*move)

    def drain(b, carry):
        @pl.when(b > 0)
        def _():
            halo(b, 0).wait_send()
            halo(b, 1).wait_send()

        forwarded(b, lambda copy: copy.wait_send())
        return carry

    lax.fori_loop(0, blocks, drain, 0)
    for s in range(segments):
        for n in range(len(chunks)):
            sent(*outcome(s, n))
    for member in range(segments):
        for n, (start, size) in enumerate(chunks):
            received(out.at[member, pl.ds(start * CELLS, size * CELLS)], o_recv.at[member, n])


def body(
    field,
    depth_kernel,
    depth_bias,
    norm_gain,
    up_weight,
    up_bias,
    down_weight,
    scale_exponent,
    live_count,
    neighbours,
    rotations,
):
    members, count = field.shape[:2]
    chans = field.shape[-1]
    hid = up_weight.shape[-1]
    segments = lax.axis_size("segment")
    devices = lax.axis_size("space")
    blocks = segments * BPS
    assert members == segments and segments % 2 == 0 and count % 2 == 0
    assert BPS % 2 == 0 and devices % 2 == 0
    pairs = segments // 2
    metas = count + 8
    assert UP_BIAS + hid // chans <= PS
    smem = pl.BlockSpec(memory_space=pltpu.SMEM)
    hbm = pl.BlockSpec(memory_space=pl.ANY)
    dma = pltpu.SemaphoreType.DMA
    out = pl.pallas_call(
        functools.partial(kernel, segments, devices, blocks),
        out_shape=pltpu.VMEM((members, count * CELLS, chans), jnp.bfloat16),
        in_specs=[hbm] * 8 + [smem] + [hbm] * 2,
        out_specs=pl.BlockSpec(memory_space=pltpu.VMEM),
        scratch_shapes=[
            pltpu.VMEM((KS * KS, BPS, chans), jnp.bfloat16),
            pltpu.VMEM((BPS, chans), jnp.bfloat16),
            pltpu.VMEM((BPS, chans), jnp.bfloat16),
            pltpu.VMEM((BPS, hid), jnp.bfloat16),
            pltpu.VMEM((BPS, chans), jnp.int32),
            pltpu.VMEM(neighbours.shape, jnp.int32),
            pltpu.VMEM(rotations.shape, jnp.int32),
            pltpu.VMEM((metas, chans), jnp.int32),
            pltpu.VMEM((metas, chans), jnp.int32),
            pltpu.SMEM((metas, chans), jnp.int32),
            pltpu.VMEM((blocks + 1, count * CELLS, chans), jnp.bfloat16),
            pltpu.VMEM((blocks, 2 * CELLS, chans), jnp.bfloat16),
            pltpu.VMEM((blocks, chans, hid), jnp.bfloat16),
            pltpu.VMEM((blocks, hid, chans), jnp.bfloat16),
            pltpu.VMEM((blocks, KS + 1, PS, chans), jnp.float32),
            pltpu.VMEM((TURNS * (count + 3) * PS, PS, chans), jnp.float32),
            pltpu.VMEM((TURNS * (count + 3) * PS, PS, chans), jnp.float32),
            pltpu.VMEM((count * EXT, WIDE, chans), jnp.float32),
            dma((3,)),
            dma((BPS, 3 + 4 * (pairs - 1))),
            dma((3, blocks)),
            dma((blocks,)),
            dma((blocks, 2)),
            dma((blocks, 2)),
            dma((4,)),
            dma((2,)),
            dma((segments, 4)),
            dma((members, 4)),
            dma((7,)),
        ],
        compiler_params=pltpu.CompilerParams(
            collective_id=0, has_side_effects=True, vmem_limit_bytes=60 * 2**20
        ),
    )(
        field.reshape(members, count * CELLS, chans),
        jnp.transpose(depth_kernel, (1, 0, 2)),
        depth_bias,
        norm_gain,
        up_weight,
        up_bias,
        down_weight,
        scale_exponent,
        live_count,
        neighbours,
        rotations,
    )
    return out.reshape((1,) + field.shape)


def solution(mesh):
    in_specs = (
        P(None, "space", None, None, None),
        P("segment", None, None),
        P("segment", None),
        P("segment", None),
        P("segment", None, None),
        P("segment", None),
        P("segment", None, None),
        P("segment", None),
        P("space"),
        P("space", None),
        P("space", None),
    )
    out_specs = P("segment", None, "space", None, None, None)
    return jax.shard_map(body, mesh=mesh, in_specs=in_specs, out_specs=out_specs, check_vma=False)
```

```python
import functools

import jax
import jax.numpy as jnp
import numpy as np
from jax import lax
from jax.experimental import pallas as pl
from jax.experimental.pallas import tpu as pltpu
from jax.sharding import PartitionSpec as P

KS = 7
BPS = 2
EDGE = 1
MARGIN = KS // 2
PS = 8
CELLS = PS * PS
EXT = PS + 2 * MARGIN
WIDE = 3 * PS
TURNS = 4
MESH = pl.DeviceIdType.MESH
HOLDERS = {8: (2, 0, 1, 3, 5, 7, 6, 4)}

BIAS = 0
GAIN = 1
SCALE = 2
UP_BIAS = 3


def bases(neighbours, rotations, place, devices, tiles):
    count = neighbours.shape[0]
    local = neighbours - place * count
    following = lax.rem(place + 1, devices) * count
    slot = jnp.where(neighbours == following, count + 1, count)
    slot = jnp.where(jnp.logical_and(local >= 0, local < count), local, slot)
    slot = jnp.where(neighbours < 0, count + 2, slot)
    return (rotations * tiles + slot) * PS


def lookup(table, index):
    value = index
    for k, entry in enumerate(table):
        if entry != k:
            value = jnp.where(index == k, entry, value)
    return value


def position(space, devices):
    return lookup([HOLDERS.get(devices, range(devices)).index(k) for k in range(devices)], space)


def holder(place, devices):
    return lookup(HOLDERS.get(devices, range(devices)), place)


def gelu2(x):
    return x * (1.0 + lax.erf(x * np.float32(0.5**0.5)))


def kernel(
    segments,
    devices,
    blocks,
    field,
    taps,
    bias,
    gain,
    up,
    up_bias,
    down,
    scale,
    live_count,
    neighbours,
    rotations,
    out,
    v_taps,
    v_bias,
    v_gain,
    v_up_bias,
    v_scale,
    v_neighbours,
    v_rotations,
    meta,
    here,
    links,
    win,
    edges,
    ups,
    downs,
    small,
    tiles_a,
    tiles_b,
    ext,
    loc_sem,
    own_sem,
    w_recv,
    fwd_sem,
    h_send,
    h_recv,
    f_send,
    f_recv,
    o_send,
    o_recv,
    in_sem,
):
    space = lax.axis_index("space")
    me = lax.axis_index("segment")
    rows = win.shape[1]
    count = rows // CELLS
    tiles = count + 3
    place = position(space, devices)
    following = lax.rem(place + 1, devices)
    preceding = lax.rem(place + devices - 1, devices)
    after = holder(following, devices)
    before = holder(preceding, devices)
    core = lax.rem(me, 2)
    pair = me // 2
    partner = pair * 2 + (1 - core)
    pairs = segments // 2
    mine = me * BPS

    barrier = pltpu.get_barrier_semaphore()
    new_home = holder(space, devices)

    def greet(where, segment):
        other = jnp.logical_or(where != space, segment != me)

        @pl.when(other)
        def _():
            pl.semaphore_signal(
                barrier, inc=1, device_id=(where, segment), device_id_type=MESH
            )

        return jnp.where(other, 1, 0)

    greetings = 0
    for where in (before, after, preceding, place, following):
        greetings += greet(where, me)
    for step in range(1, segments):
        greetings += greet(space, lax.rem(me + step, segments))
    for segment in range(segments):
        greetings += greet(new_home, segment)

    own_up = pltpu.make_async_copy(up, ups.at[pl.ds(mine, BPS)], loc_sem.at[0])
    own_up.start()
    own_down = pltpu.make_async_copy(down, downs.at[pl.ds(mine, BPS)], loc_sem.at[1])
    own_down.start()
    loads = [
        pltpu.make_async_copy(src, dst, in_sem.at[n])
        for n, (src, dst) in enumerate(
            (
                (neighbours, v_neighbours),
                (rotations, v_rotations),
                (taps, v_taps),
                (bias, v_bias),
                (gain, v_gain),
                (up_bias, v_up_bias),
                (scale, v_scale),
            )
        )
    ]
    for load in loads:
        load.start()
    order = [count - 1, *range(count - 1)]
    half = 2 + (count - 2) // 2
    hid = up_bias.shape[1]
    chans = up.shape[1]
    for load in loads:
        load.wait()
    meta[...] = jnp.full(meta.shape, live_count[0], jnp.int32)
    meta[0:count, 0:8] = bases(v_neighbours[...], v_rotations[...], space, devices, tiles)
    for k in range(BPS):
        for row in range(KS):
            small[mine + k, row, 0:KS, :] = v_taps[
                row * KS : (row + 1) * KS, k, :
            ].astype(jnp.float32)
        small[mine + k, KS, BIAS : BIAS + 1, :] = v_bias[k : k + 1, :].astype(jnp.float32)
        small[mine + k, KS, GAIN : GAIN + 1, :] = v_gain[k : k + 1, :].astype(jnp.float32)
        small[mine + k, KS, SCALE : SCALE + 1, :] = 0.5 * jnp.exp2(
            v_scale[k : k + 1, :].astype(jnp.float32) * 0.5
        )
        for q in range(hid // chans):
            small[mine + k, KS, UP_BIAS + q : UP_BIAS + q + 1, :] = v_up_bias[
                k : k + 1, q * chans : (q + 1) * chans
            ].astype(jnp.float32)

    def flat(ref):
        return ref.reshape(ref.shape[0] * PS, chans)

    empty = jnp.zeros((CELLS, chans), jnp.float32)
    for turn in range(TURNS):
        at = (turn * tiles + count + 2) * CELLS
        flat(tiles_a)[at : at + CELLS, :] = empty
        flat(tiles_b)[at : at + CELLS, :] = empty
    pl.semaphore_wait(barrier, greetings)

    def send(src, dst, where, segment, send_sem, recv_sem):
        same = jnp.logical_and(where == space, segment == me)

        @pl.when(same)
        def _():
            pltpu.make_async_copy(src, dst, recv_sem).start()

        @pl.when(jnp.logical_not(same))
        def _():
            pltpu.make_async_remote_copy(
                src_ref=src,
                dst_ref=dst,
                send_sem=send_sem,
                recv_sem=recv_sem,
                device_id=(where, segment),
                device_id_type=MESH,
            ).start()

    def sent(src, dst, where, segment, send_sem, recv_sem):
        @pl.when(jnp.logical_not(jnp.logical_and(where == space, segment == me)))
        def _():
            pltpu.make_async_remote_copy(
                src_ref=src,
                dst_ref=dst,
                send_sem=send_sem,
                recv_sem=recv_sem,
                device_id=(where, segment),
                device_id_type=MESH,
            ).wait_send()

    def received(ref, recv_sem):
        pltpu.make_async_copy(ref, ref, recv_sem).wait()

    first = pl.ds(0, CELLS)
    last = pl.ds(rows - CELLS, CELLS)

    def lower(b):
        return edges.at[b, pl.ds(0, CELLS)]

    def upper(b):
        return edges.at[b, pl.ds(CELLS, CELLS)]

    ahead = holder(lax.rem(space + 1, devices), devices)
    behind = holder(lax.rem(space + devices - 1, devices), devices)
    moves = (
        (meta, here, new_home, me, f_send.at[0], f_recv.at[0]),
        (field.at[me, last], lower(0), ahead, me, f_send.at[1], h_recv.at[0, 0]),
        (field.at[me, first], upper(0), behind, me, f_send.at[2], h_recv.at[0, 1]),
        (field.at[me], win.at[0], new_home, me, f_send.at[3], f_recv.at[1]),
    )

    def halo(b, side):
        if side == 0:
            src, dst, to = win.at[b, last], lower(b), after
        else:
            src, dst, to = win.at[b, first], upper(b), before
        return pltpu.make_async_remote_copy(
            src_ref=src,
            dst_ref=dst,
            send_sem=h_send.at[b, side],
            recv_sem=h_recv.at[b, side],
            device_id=(to, me),
            device_id_type=MESH,
        )

    def piece(kind, b, to, send_sem):
        ref = (small, ups, downs)[kind].at[b]
        return pltpu.make_async_remote_copy(
            src_ref=ref,
            dst_ref=ref,
            send_sem=send_sem,
            recv_sem=w_recv.at[kind, b],
            device_id=(space, to),
            device_id_type=MESH,
        )

    def to_partner():
        return [
            piece(kind, mine + k, partner, own_sem.at[k, kind])
            for k in range(BPS)
            for kind in range(3)
        ]

    def to_pairs(k):
        copies = []
        for step in range(1, pairs):
            other = lax.rem(pair + step, pairs) * 2
            at = 3 + (step - 1) * 4
            copies.append(piece(0, mine + k, other, own_sem.at[k, at]))
            copies.append(piece(1, mine + k, other, own_sem.at[k, at + 2]))
            copies.append(piece(2, mine + k, other + 1, own_sem.at[k, at + 3]))
        return copies

    def turn_of(k):
        if k == 0:
            late = jnp.where(core == 0, 1, 4)
        else:
            late = jnp.where(core == 0, 2, 5)
        return jnp.where(pair == 0, jnp.where(core == 0, -1, k + 1), 2 * BPS * (pair - 1) + late)

    def forwarded(b, act):
        foreign = b // (2 * BPS) != pair

        @pl.when(jnp.logical_and(foreign, core == 0))
        def _():
            act(piece(0, b, partner, fwd_sem.at[1, b]))
            act(piece(1, b, partner, fwd_sem.at[0, b]))

        @pl.when(jnp.logical_and(foreign, core == 1))
        def _():
            act(piece(2, b, partner, fwd_sem.at[0, b]))

    def forward(b):
        def act(copy):
            copy.wait_recv()
            copy.start()

        forwarded(b, act)

    def arrive(b):
        owner = b // BPS
        foreign = b // (2 * BPS) != pair

        relayed = jnp.logical_and(foreign, core == 0)

        @pl.when(jnp.logical_and(owner != me, jnp.logical_not(relayed)))
        def _():
            piece(0, b, partner, fwd_sem.at[0, b]).wait_recv()

        @pl.when(owner == partner)
        def _():
            piece(1, b, partner, fwd_sem.at[0, b]).wait_recv()
            piece(2, b, partner, fwd_sem.at[0, b]).wait_recv()

        @pl.when(jnp.logical_and(foreign, core == 0))
        def _():
            piece(2, b, partner, fwd_sem.at[0, b]).wait_recv()

        @pl.when(jnp.logical_and(foreign, core == 1))
        def _():
            piece(1, b, partner, fwd_sem.at[0, b]).wait_recv()

    chunks = ((count - 1, 1), (0, 1), (1, half - 2), (half - 1, count - half))

    def outcome(s, n):
        at = pl.ds(chunks[n][0] * CELLS, chunks[n][1] * CELLS)
        return (
            win.at[BPS * (s + 1), at],
            out.at[me, at],
            place,
            s,
            o_send.at[s, n],
            o_recv.at[me, n],
        )

    def spread(dst, slot, cells):
        dst = flat(dst)
        at = [(turn * tiles + slot) * CELLS for turn in range(TURNS)]
        for i in range(PS):
            row = cells[i * PS : (i + 1) * PS]
            dst[at[0] + i * PS : at[0] + (i + 1) * PS, :] = row
            dst[pl.ds(at[3] + PS - 1 - i, PS, stride=PS), :] = row
        for old, new in ((0, 1), (1, 2)):
            for j in range(PS):
                to = at[new] + (PS - 1 - j) * PS
                dst[to : to + PS, :] = dst[pl.ds(at[old] + j, PS, stride=PS), :]

    def middle(g):
        return (slice(g * EXT + MARGIN, g * EXT + MARGIN + PS), slice(PS, 2 * PS))

    def enter(dst, g, cells):
        spread(dst, g, cells)
        ext[middle(g)] = cells.reshape(PS, PS, chans)

    def margins(src, g):
        for d in range(8):
            band_i, band_j = ((0, 0), (0, 1), (0, 2), (1, 0), (1, 2), (2, 0), (2, 1), (2, 2))[d]
            base = links[g, d]
            if band_i == 0:
                lines = [(PS - MARGIN + i, i) for i in range(MARGIN)]
            elif band_i == 1:
                lines = [(i, MARGIN + i) for i in range(PS)]
            else:
                lines = [(i, MARGIN + PS + i) for i in range(MARGIN)]
            for i, to in lines:
                ext[g * EXT + to, band_j * PS : (band_j + 1) * PS, :] = src[base + i]

    def convolve(b, places):
        def line(a, total):
            for e in range(KS):
                window = jnp.concatenate(
                    [
                        ext[pl.ds(g * EXT + a, PS), PS - MARGIN + e : 2 * PS - MARGIN + e, :]
                        for g in places
                    ],
                    axis=0,
                )
                total = total + window * small[b, a, e : e + 1, :][None]
            return total

        start = small[b, KS, BIAS : BIAS + 1, :][None]
        start = jnp.broadcast_to(start, (len(places) * PS, PS, chans))
        total = lax.fori_loop(0, KS, line, start).reshape(-1, chans)
        centred = total - jnp.mean(total, axis=-1, keepdims=True)
        variance = jnp.mean(centred * centred, axis=-1, keepdims=True)
        scaled = centred * lax.rsqrt(variance + 1e-06) * small[b, KS, GAIN : GAIN + 1, :]
        return scaled.astype(jnp.bfloat16)

    def group(b, begin, end):
        normed = convolve(b, order[begin:end])
        wide = jnp.concatenate(
            [small[b, KS, UP_BIAS + q : UP_BIAS + q + 1, :] for q in range(hid // chans)], axis=1
        )
        hidden = jnp.dot(normed, ups[b], preferred_element_type=jnp.float32) + wide
        hidden = gelu2(hidden).astype(jnp.bfloat16)
        branch = jnp.dot(hidden, downs[b], preferred_element_type=jnp.float32)
        branch = branch * small[b, KS, SCALE : SCALE + 1, :]
        for n in range(begin, end):
            g = order[n]
            alive = jnp.logical_or(g < links[count, 0] - EDGE, g >= count - EDGE)
            alive = jnp.where(alive, 1.0, 0.0)
            old = ext[middle(g)].reshape(CELLS, chans)
            state = old + branch[(n - begin) * CELLS : (n - begin + 1) * CELLS]
            state = (state * alive).astype(jnp.bfloat16)
            win[b + 1, g * CELLS : (g + 1) * CELLS, :] = state

    def settle(b, begin, end, dst):
        for n in range(begin, end):
            g = order[n]
            enter(dst, g, win[b + 1, g * CELLS : (g + 1) * CELLS, :].astype(jnp.float32))

    for move in moves:
        send(*move)
    own_up.wait()
    own_down.wait()

    opening = me == 0

    @pl.when(opening)
    def _():
        for copy in to_pairs(0):
            copy.start()

    for copy in to_partner():
        copy.start()

    @pl.when(opening)
    def _():
        for copy in to_pairs(1):
            copy.start()

    forward(0)

    received(here, f_recv.at[0])
    table = pltpu.make_async_copy(here, links, loc_sem.at[2])
    table.start()
    received(win.at[0], f_recv.at[1])
    for g in range(count):
        enter(tiles_a, g, win[0, g * CELLS : (g + 1) * CELLS, :].astype(jnp.float32))
    table.wait()

    def layer(s, part):
        b = s * BPS + part
        src, dst = (tiles_a, tiles_b) if part % 2 == 0 else (tiles_b, tiles_a)
        arrive(b)
        for k in range(BPS):

            @pl.when(b == turn_of(k))
            def _():
                for copy in to_pairs(k):
                    copy.start()

        received(lower(b), h_recv.at[b, 0])
        received(upper(b), h_recv.at[b, 1])
        for side in range(2):
            tile = edges[b, side * CELLS : (side + 1) * CELLS, :].astype(jnp.float32)
            spread(src, count + side, tile)
        for n in range(2):
            margins(src, order[n])
        group(b, 0, 2)

        @pl.when(b < blocks - 1)
        def _():
            halo(b + 1, 0).start()
            halo(b + 1, 1).start()

        ends = part == BPS - 1
        if ends:
            send(*outcome(s, 0))
            send(*outcome(s, 1))
        settle(b, 0, 2, dst)
        for n in range(2, count):
            margins(src, order[n])
        group(b, 2, half)
        if ends:
            send(*outcome(s, 2))
        group(b, half, count)
        if ends:
            send(*outcome(s, 3))
        settle(b, 2, count, dst)

        @pl.when(b < blocks - 1)
        def _():
            forward(b + 1)

    def section(s, carry):
        for part in range(BPS):
            layer(s, part)
        return carry

    lax.fori_loop(0, segments, section, 0)

    for copy in to_partner() + to_pairs(0) + to_pairs(1):
        copy.wait_send()

    for move in moves:
        sent(*move)

    def drain(b, carry):
        @pl.when(b > 0)
        def _():
            halo(b, 0).wait_send()
            halo(b, 1).wait_send()

        forwarded(b, lambda copy: copy.wait_send())
        return carry

    lax.fori_loop(0, blocks, drain, 0)
    for s in range(segments):
        for n in range(len(chunks)):
            sent(*outcome(s, n))
    for member in range(segments):
        for n, (start, size) in enumerate(chunks):
            received(out.at[member, pl.ds(start * CELLS, size * CELLS)], o_recv.at[member, n])


def body(
    field,
    depth_kernel,
    depth_bias,
    norm_gain,
    up_weight,
    up_bias,
    down_weight,
    scale_exponent,
    live_count,
    neighbours,
    rotations,
):
    members, count = field.shape[:2]
    chans = field.shape[-1]
    hid = up_weight.shape[-1]
    segments = lax.axis_size("segment")
    devices = lax.axis_size("space")
    blocks = segments * BPS
    assert members == segments and segments % 2 == 0 and count % 2 == 0
    assert BPS == 2 and devices % 2 == 0
    pairs = segments // 2
    metas = count + 8
    assert UP_BIAS + hid // chans <= PS
    smem = pl.BlockSpec(memory_space=pltpu.SMEM)
    hbm = pl.BlockSpec(memory_space=pl.ANY)
    dma = pltpu.SemaphoreType.DMA
    out = pl.pallas_call(
        functools.partial(kernel, segments, devices, blocks),
        out_shape=pltpu.VMEM((members, count * CELLS, chans), jnp.bfloat16),
        in_specs=[hbm] * 8 + [smem] + [hbm] * 2,
        out_specs=pl.BlockSpec(memory_space=pltpu.VMEM),
        scratch_shapes=[
            pltpu.VMEM((KS * KS, BPS, chans), jnp.bfloat16),
            pltpu.VMEM((BPS, chans), jnp.bfloat16),
            pltpu.VMEM((BPS, chans), jnp.bfloat16),
            pltpu.VMEM((BPS, hid), jnp.bfloat16),
            pltpu.VMEM((BPS, chans), jnp.int32),
            pltpu.VMEM(neighbours.shape, jnp.int32),
            pltpu.VMEM(rotations.shape, jnp.int32),
            pltpu.VMEM((metas, chans), jnp.int32),
            pltpu.VMEM((metas, chans), jnp.int32),
            pltpu.SMEM((metas, chans), jnp.int32),
            pltpu.VMEM((blocks + 1, count * CELLS, chans), jnp.bfloat16),
            pltpu.VMEM((blocks, 2 * CELLS, chans), jnp.bfloat16),
            pltpu.VMEM((blocks, chans, hid), jnp.bfloat16),
            pltpu.VMEM((blocks, hid, chans), jnp.bfloat16),
            pltpu.VMEM((blocks, KS + 1, PS, chans), jnp.float32),
            pltpu.VMEM((TURNS * (count + 3) * PS, PS, chans), jnp.float32),
            pltpu.VMEM((TURNS * (count + 3) * PS, PS, chans), jnp.float32),
            pltpu.VMEM((count * EXT, WIDE, chans), jnp.float32),
            dma((3,)),
            dma((BPS, 3 + 4 * (pairs - 1))),
            dma((3, blocks)),
            dma((2, blocks)),
            dma((blocks, 2)),
            dma((blocks, 2)),
            dma((4,)),
            dma((2,)),
            dma((segments, 4)),
            dma((members, 4)),
            dma((7,)),
        ],
        compiler_params=pltpu.CompilerParams(
            collective_id=0, has_side_effects=True, vmem_limit_bytes=60 * 2**20
        ),
    )(
        field.reshape(members, count * CELLS, chans),
        jnp.transpose(depth_kernel, (1, 0, 2)),
        depth_bias,
        norm_gain,
        up_weight,
        up_bias,
        down_weight,
        scale_exponent,
        live_count,
        neighbours,
        rotations,
    )
    return out.reshape((1,) + field.shape)


def solution(mesh):
    in_specs = (
        P(None, "space", None, None, None),
        P("segment", None, None),
        P("segment", None),
        P("segment", None),
        P("segment", None, None),
        P("segment", None),
        P("segment", None, None),
        P("segment", None),
        P("space"),
        P("space", None),
        P("space", None),
    )
    out_specs = P("segment", None, "space", None, None, None)
    return jax.shard_map(body, mesh=mesh, in_specs=in_specs, out_specs=out_specs, check_vma=False)
```

```python
import functools

import jax
import jax.numpy as jnp
import numpy as np
from jax import lax
from jax.experimental import pallas as pl
from jax.experimental.pallas import tpu as pltpu
from jax.sharding import PartitionSpec as P

KS = 7
BPS = 2
EDGE = 1
MARGIN = KS // 2
PS = 8
CELLS = PS * PS
EXT = PS + 2 * MARGIN
WIDE = 3 * PS
TURNS = 4
MESH = pl.DeviceIdType.MESH
HOLDERS = {8: (2, 0, 1, 3, 5, 7, 6, 4)}

BIAS = 0
GAIN = 1
SCALE = 2
UP_BIAS = 3


def bases(neighbours, rotations, place, devices, tiles):
    count = neighbours.shape[0]
    local = neighbours - place * count
    following = lax.rem(place + 1, devices) * count
    slot = jnp.where(neighbours == following, count + 1, count)
    slot = jnp.where(jnp.logical_and(local >= 0, local < count), local, slot)
    slot = jnp.where(neighbours < 0, count + 2, slot)
    return (rotations * tiles + slot) * PS


def lookup(table, index):
    value = index
    for k, entry in enumerate(table):
        if entry != k:
            value = jnp.where(index == k, entry, value)
    return value


def position(space, devices):
    return lookup([HOLDERS.get(devices, range(devices)).index(k) for k in range(devices)], space)


def holder(place, devices):
    return lookup(HOLDERS.get(devices, range(devices)), place)


def gelu2(x):
    return x * (1.0 + lax.erf(x * np.float32(0.5**0.5)))


def kernel(
    segments,
    devices,
    blocks,
    field,
    taps,
    bias,
    gain,
    up,
    up_bias,
    down,
    scale,
    live_count,
    neighbours,
    rotations,
    out,
    v_taps,
    v_bias,
    v_gain,
    v_up_bias,
    v_scale,
    v_neighbours,
    v_rotations,
    meta,
    here,
    links,
    win,
    edges,
    ups,
    downs,
    small,
    tiles_a,
    tiles_b,
    ext,
    loc_sem,
    own_sem,
    w_recv,
    fwd_sem,
    h_send,
    h_recv,
    f_send,
    f_recv,
    o_send,
    o_recv,
    in_sem,
):
    space = lax.axis_index("space")
    me = lax.axis_index("segment")
    rows = win.shape[1]
    count = rows // CELLS
    tiles = count + 3
    place = position(space, devices)
    following = lax.rem(place + 1, devices)
    preceding = lax.rem(place + devices - 1, devices)
    after = holder(following, devices)
    before = holder(preceding, devices)
    core = lax.rem(me, 2)
    pair = me // 2
    partner = pair * 2 + (1 - core)
    pairs = segments // 2
    mine = me * BPS

    barrier = pltpu.get_barrier_semaphore()
    new_home = holder(space, devices)

    def greet(where, segment):
        other = jnp.logical_or(where != space, segment != me)

        @pl.when(other)
        def _():
            pl.semaphore_signal(
                barrier, inc=1, device_id=(where, segment), device_id_type=MESH
            )

        return jnp.where(other, 1, 0)

    greetings = 0
    for where in (before, after, preceding, place, following):
        greetings += greet(where, me)
    for step in range(1, segments):
        greetings += greet(space, lax.rem(me + step, segments))
    for segment in range(segments):
        greetings += greet(new_home, segment)

    own_up = pltpu.make_async_copy(up, ups.at[pl.ds(mine, BPS)], loc_sem.at[0])
    own_up.start()
    own_down = pltpu.make_async_copy(down, downs.at[pl.ds(mine, BPS)], loc_sem.at[1])
    own_down.start()
    loads = [
        pltpu.make_async_copy(src, dst, in_sem.at[n])
        for n, (src, dst) in enumerate(
            (
                (neighbours, v_neighbours),
                (rotations, v_rotations),
                (taps, v_taps),
                (bias, v_bias),
                (gain, v_gain),
                (up_bias, v_up_bias),
                (scale, v_scale),
            )
        )
    ]
    for load in loads:
        load.start()
    order = [count - 1, *range(count - 1)]
    half = 2 + (count - 2) // 2
    hid = up_bias.shape[1]
    chans = up.shape[1]
    for load in loads:
        load.wait()
    meta[...] = jnp.full(meta.shape, live_count[0], jnp.int32)
    meta[0:count, 0:8] = bases(v_neighbours[...], v_rotations[...], space, devices, tiles)
    for k in range(BPS):
        for row in range(KS):
            small[mine + k, row, 0:KS, :] = v_taps[
                row * KS : (row + 1) * KS, k, :
            ].astype(jnp.float32)
        small[mine + k, KS, BIAS : BIAS + 1, :] = v_bias[k : k + 1, :].astype(jnp.float32)
        small[mine + k, KS, GAIN : GAIN + 1, :] = v_gain[k : k + 1, :].astype(jnp.float32)
        small[mine + k, KS, SCALE : SCALE + 1, :] = 0.5 * jnp.exp2(
            v_scale[k : k + 1, :].astype(jnp.float32) * 0.5
        )
        for q in range(hid // chans):
            small[mine + k, KS, UP_BIAS + q : UP_BIAS + q + 1, :] = v_up_bias[
                k : k + 1, q * chans : (q + 1) * chans
            ].astype(jnp.float32)

    def flat(ref):
        return ref.reshape(ref.shape[0] * PS, chans)

    empty = jnp.zeros((CELLS, chans), jnp.float32)
    for turn in range(TURNS):
        at = (turn * tiles + count + 2) * CELLS
        flat(tiles_a)[at : at + CELLS, :] = empty
        flat(tiles_b)[at : at + CELLS, :] = empty
    pl.semaphore_wait(barrier, greetings)

    def send(src, dst, where, segment, send_sem, recv_sem):
        same = jnp.logical_and(where == space, segment == me)

        @pl.when(same)
        def _():
            pltpu.make_async_copy(src, dst, recv_sem).start()

        @pl.when(jnp.logical_not(same))
        def _():
            pltpu.make_async_remote_copy(
                src_ref=src,
                dst_ref=dst,
                send_sem=send_sem,
                recv_sem=recv_sem,
                device_id=(where, segment),
                device_id_type=MESH,
            ).start()

    def sent(src, dst, where, segment, send_sem, recv_sem):
        @pl.when(jnp.logical_not(jnp.logical_and(where == space, segment == me)))
        def _():
            pltpu.make_async_remote_copy(
                src_ref=src,
                dst_ref=dst,
                send_sem=send_sem,
                recv_sem=recv_sem,
                device_id=(where, segment),
                device_id_type=MESH,
            ).wait_send()

    def received(ref, recv_sem):
        pltpu.make_async_copy(ref, ref, recv_sem).wait()

    first = pl.ds(0, CELLS)
    last = pl.ds(rows - CELLS, CELLS)

    def lower(b):
        return edges.at[b, pl.ds(0, CELLS)]

    def upper(b):
        return edges.at[b, pl.ds(CELLS, CELLS)]

    ahead = holder(lax.rem(space + 1, devices), devices)
    behind = holder(lax.rem(space + devices - 1, devices), devices)
    moves = (
        (meta, here, new_home, me, f_send.at[0], f_recv.at[0]),
        (field.at[me, last], lower(0), ahead, me, f_send.at[1], h_recv.at[0, 0]),
        (field.at[me, first], upper(0), behind, me, f_send.at[2], h_recv.at[0, 1]),
        (field.at[me], win.at[0], new_home, me, f_send.at[3], f_recv.at[1]),
    )

    def halo(b, side):
        if side == 0:
            src, dst, to = win.at[b, last], lower(b), after
        else:
            src, dst, to = win.at[b, first], upper(b), before
        return pltpu.make_async_remote_copy(
            src_ref=src,
            dst_ref=dst,
            send_sem=h_send.at[b, side],
            recv_sem=h_recv.at[b, side],
            device_id=(to, me),
            device_id_type=MESH,
        )

    def piece(kind, b, to, send_sem):
        ref = (small, ups, downs)[kind].at[b]
        return pltpu.make_async_remote_copy(
            src_ref=ref,
            dst_ref=ref,
            send_sem=send_sem,
            recv_sem=w_recv.at[kind, b],
            device_id=(space, to),
            device_id_type=MESH,
        )

    def to_partner():
        return [
            piece(kind, mine + k, partner, own_sem.at[k, kind])
            for k in range(BPS)
            for kind in range(3)
        ]

    def to_pairs(k):
        copies = []
        for step in range(1, pairs):
            other = lax.rem(pair + step, pairs) * 2
            at = 3 + (step - 1) * 4
            copies.append(piece(0, mine + k, other, own_sem.at[k, at]))
            copies.append(piece(1, mine + k, other, own_sem.at[k, at + 2]))
            copies.append(piece(2, mine + k, other + 1, own_sem.at[k, at + 3]))
        return copies

    def turn_of(k):
        if k == 0:
            late = jnp.where(core == 0, 1, 4)
        else:
            late = jnp.where(core == 0, 2, 5)
        return jnp.where(pair == 0, jnp.where(core == 0, -1, k + 1), 2 * BPS * (pair - 1) + late)

    def forwarded(b, act):
        foreign = b // (2 * BPS) != pair

        @pl.when(jnp.logical_and(foreign, core == 0))
        def _():
            act(piece(0, b, partner, fwd_sem.at[1, b]))
            act(piece(1, b, partner, fwd_sem.at[0, b]))

        @pl.when(jnp.logical_and(foreign, core == 1))
        def _():
            act(piece(2, b, partner, fwd_sem.at[0, b]))

    def forward(b):
        def act(copy):
            copy.wait_recv()
            copy.start()

        forwarded(b, act)

    def arrive(b):
        owner = b // BPS
        foreign = b // (2 * BPS) != pair

        relayed = jnp.logical_and(foreign, core == 0)

        @pl.when(jnp.logical_and(owner != me, jnp.logical_not(relayed)))
        def _():
            piece(0, b, partner, fwd_sem.at[0, b]).wait_recv()

    def arrive_wide(b):
        owner = b // BPS
        foreign = b // (2 * BPS) != pair

        @pl.when(owner == partner)
        def _():
            piece(1, b, partner, fwd_sem.at[0, b]).wait_recv()
            piece(2, b, partner, fwd_sem.at[0, b]).wait_recv()

        @pl.when(jnp.logical_and(foreign, core == 0))
        def _():
            piece(2, b, partner, fwd_sem.at[0, b]).wait_recv()

        @pl.when(jnp.logical_and(foreign, core == 1))
        def _():
            piece(1, b, partner, fwd_sem.at[0, b]).wait_recv()

    chunks = ((count - 1, 1), (0, 1), (1, half - 2), (half - 1, count - half))

    def outcome(s, n):
        at = pl.ds(chunks[n][0] * CELLS, chunks[n][1] * CELLS)
        return (
            win.at[BPS * (s + 1), at],
            out.at[me, at],
            place,
            s,
            o_send.at[s, n],
            o_recv.at[me, n],
        )

    def spread(dst, slot, cells):
        dst = flat(dst)
        at = [(turn * tiles + slot) * CELLS for turn in range(TURNS)]
        for i in range(PS):
            row = cells[i * PS : (i + 1) * PS]
            dst[at[0] + i * PS : at[0] + (i + 1) * PS, :] = row
            dst[pl.ds(at[3] + PS - 1 - i, PS, stride=PS), :] = row
        for old, new in ((0, 1), (1, 2)):
            for j in range(PS):
                to = at[new] + (PS - 1 - j) * PS
                dst[to : to + PS, :] = dst[pl.ds(at[old] + j, PS, stride=PS), :]

    def middle(g):
        return (slice(g * EXT + MARGIN, g * EXT + MARGIN + PS), slice(PS, 2 * PS))

    def enter(dst, g, cells):
        spread(dst, g, cells)
        ext[middle(g)] = cells.reshape(PS, PS, chans)

    def margins(src, g):
        for d in range(8):
            band_i, band_j = ((0, 0), (0, 1), (0, 2), (1, 0), (1, 2), (2, 0), (2, 1), (2, 2))[d]
            base = links[g, d]
            if band_i == 0:
                lines = [(PS - MARGIN + i, i) for i in range(MARGIN)]
            elif band_i == 1:
                lines = [(i, MARGIN + i) for i in range(PS)]
            else:
                lines = [(i, MARGIN + PS + i) for i in range(MARGIN)]
            for i, to in lines:
                ext[g * EXT + to, band_j * PS : (band_j + 1) * PS, :] = src[base + i]

    def convolve(b, places):
        def line(a, total):
            for e in range(KS):
                window = jnp.concatenate(
                    [
                        ext[pl.ds(g * EXT + a, PS), PS - MARGIN + e : 2 * PS - MARGIN + e, :]
                        for g in places
                    ],
                    axis=0,
                )
                total = total + window * small[b, a, e : e + 1, :][None]
            return total

        start = small[b, KS, BIAS : BIAS + 1, :][None]
        start = jnp.broadcast_to(start, (len(places) * PS, PS, chans))
        total = lax.fori_loop(0, KS, line, start).reshape(-1, chans)
        centred = total - jnp.mean(total, axis=-1, keepdims=True)
        variance = jnp.mean(centred * centred, axis=-1, keepdims=True)
        scaled = centred * lax.rsqrt(variance + 1e-06) * small[b, KS, GAIN : GAIN + 1, :]
        return scaled.astype(jnp.bfloat16)

    def group(b, begin, end):
        normed = convolve(b, order[begin:end])
        if begin == 0:
            arrive_wide(b)
        wide = jnp.concatenate(
            [small[b, KS, UP_BIAS + q : UP_BIAS + q + 1, :] for q in range(hid // chans)], axis=1
        )
        hidden = jnp.dot(normed, ups[b], preferred_element_type=jnp.float32) + wide
        hidden = gelu2(hidden).astype(jnp.bfloat16)
        branch = jnp.dot(hidden, downs[b], preferred_element_type=jnp.float32)
        branch = branch * small[b, KS, SCALE : SCALE + 1, :]
        for n in range(begin, end):
            g = order[n]
            alive = jnp.logical_or(g < links[count, 0] - EDGE, g >= count - EDGE)
            alive = jnp.where(alive, 1.0, 0.0)
            old = ext[middle(g)].reshape(CELLS, chans)
            state = old + branch[(n - begin) * CELLS : (n - begin + 1) * CELLS]
            state = (state * alive).astype(jnp.bfloat16)
            win[b + 1, g * CELLS : (g + 1) * CELLS, :] = state

    def settle(b, begin, end, dst):
        for n in range(begin, end):
            g = order[n]
            enter(dst, g, win[b + 1, g * CELLS : (g + 1) * CELLS, :].astype(jnp.float32))

    for move in moves:
        send(*move)
    own_up.wait()
    own_down.wait()

    opening = me == 0

    @pl.when(opening)
    def _():
        for copy in to_pairs(0):
            copy.start()

    for copy in to_partner():
        copy.start()

    @pl.when(opening)
    def _():
        for copy in to_pairs(1):
            copy.start()

    forward(0)

    received(here, f_recv.at[0])
    table = pltpu.make_async_copy(here, links, loc_sem.at[2])
    table.start()
    received(win.at[0], f_recv.at[1])
    for g in range(count):
        enter(tiles_a, g, win[0, g * CELLS : (g + 1) * CELLS, :].astype(jnp.float32))
    table.wait()

    def layer(s, part):
        b = s * BPS + part
        src, dst = (tiles_a, tiles_b) if part % 2 == 0 else (tiles_b, tiles_a)
        arrive(b)
        for k in range(BPS):

            @pl.when(b == turn_of(k))
            def _():
                for copy in to_pairs(k):
                    copy.start()

        received(lower(b), h_recv.at[b, 0])
        received(upper(b), h_recv.at[b, 1])
        for side in range(2):
            tile = edges[b, side * CELLS : (side + 1) * CELLS, :].astype(jnp.float32)
            spread(src, count + side, tile)
        for n in range(2):
            margins(src, order[n])
        group(b, 0, 2)

        @pl.when(b < blocks - 1)
        def _():
            halo(b + 1, 0).start()
            halo(b + 1, 1).start()

        ends = part == BPS - 1
        if ends:
            send(*outcome(s, 0))
            send(*outcome(s, 1))
        settle(b, 0, 2, dst)
        for n in range(2, count):
            margins(src, order[n])
        group(b, 2, half)
        if ends:
            send(*outcome(s, 2))
        group(b, half, count)
        if ends:
            send(*outcome(s, 3))
        settle(b, 2, count, dst)

        @pl.when(b < blocks - 1)
        def _():
            forward(b + 1)

    def section(s, carry):
        for part in range(BPS):
            layer(s, part)
        return carry

    lax.fori_loop(0, segments, section, 0)

    for copy in to_partner() + to_pairs(0) + to_pairs(1):
        copy.wait_send()

    for move in moves:
        sent(*move)

    def drain(b, carry):
        @pl.when(b > 0)
        def _():
            halo(b, 0).wait_send()
            halo(b, 1).wait_send()

        forwarded(b, lambda copy: copy.wait_send())
        return carry

    lax.fori_loop(0, blocks, drain, 0)
    for s in range(segments):
        for n in range(len(chunks)):
            sent(*outcome(s, n))
    for member in range(segments):
        for n, (start, size) in enumerate(chunks):
            received(out.at[member, pl.ds(start * CELLS, size * CELLS)], o_recv.at[member, n])


def body(
    field,
    depth_kernel,
    depth_bias,
    norm_gain,
    up_weight,
    up_bias,
    down_weight,
    scale_exponent,
    live_count,
    neighbours,
    rotations,
):
    members, count = field.shape[:2]
    chans = field.shape[-1]
    hid = up_weight.shape[-1]
    segments = lax.axis_size("segment")
    devices = lax.axis_size("space")
    blocks = segments * BPS
    assert members == segments and segments % 2 == 0 and count % 2 == 0
    assert BPS == 2 and devices % 2 == 0
    pairs = segments // 2
    metas = count + 8
    assert UP_BIAS + hid // chans <= PS
    smem = pl.BlockSpec(memory_space=pltpu.SMEM)
    hbm = pl.BlockSpec(memory_space=pl.ANY)
    dma = pltpu.SemaphoreType.DMA
    out = pl.pallas_call(
        functools.partial(kernel, segments, devices, blocks),
        out_shape=pltpu.VMEM((members, count * CELLS, chans), jnp.bfloat16),
        in_specs=[hbm] * 8 + [smem] + [hbm] * 2,
        out_specs=pl.BlockSpec(memory_space=pltpu.VMEM),
        scratch_shapes=[
            pltpu.VMEM((KS * KS, BPS, chans), jnp.bfloat16),
            pltpu.VMEM((BPS, chans), jnp.bfloat16),
            pltpu.VMEM((BPS, chans), jnp.bfloat16),
            pltpu.VMEM((BPS, hid), jnp.bfloat16),
            pltpu.VMEM((BPS, chans), jnp.int32),
            pltpu.VMEM(neighbours.shape, jnp.int32),
            pltpu.VMEM(rotations.shape, jnp.int32),
            pltpu.VMEM((metas, chans), jnp.int32),
            pltpu.VMEM((metas, chans), jnp.int32),
            pltpu.SMEM((metas, chans), jnp.int32),
            pltpu.VMEM((blocks + 1, count * CELLS, chans), jnp.bfloat16),
            pltpu.VMEM((blocks, 2 * CELLS, chans), jnp.bfloat16),
            pltpu.VMEM((blocks, chans, hid), jnp.bfloat16),
            pltpu.VMEM((blocks, hid, chans), jnp.bfloat16),
            pltpu.VMEM((blocks, KS + 1, PS, chans), jnp.float32),
            pltpu.VMEM((TURNS * (count + 3) * PS, PS, chans), jnp.float32),
            pltpu.VMEM((TURNS * (count + 3) * PS, PS, chans), jnp.float32),
            pltpu.VMEM((count * EXT, WIDE, chans), jnp.float32),
            dma((3,)),
            dma((BPS, 3 + 4 * (pairs - 1))),
            dma((3, blocks)),
            dma((2, blocks)),
            dma((blocks, 2)),
            dma((blocks, 2)),
            dma((4,)),
            dma((2,)),
            dma((segments, 4)),
            dma((members, 4)),
            dma((7,)),
        ],
        compiler_params=pltpu.CompilerParams(
            collective_id=0, has_side_effects=True, vmem_limit_bytes=60 * 2**20
        ),
    )(
        field.reshape(members, count * CELLS, chans),
        jnp.transpose(depth_kernel, (1, 0, 2)),
        depth_bias,
        norm_gain,
        up_weight,
        up_bias,
        down_weight,
        scale_exponent,
        live_count,
        neighbours,
        rotations,
    )
    return out.reshape((1,) + field.shape)


def solution(mesh):
    in_specs = (
        P(None, "space", None, None, None),
        P("segment", None, None),
        P("segment", None),
        P("segment", None),
        P("segment", None, None),
        P("segment", None),
        P("segment", None, None),
        P("segment", None),
        P("space"),
        P("space", None),
        P("space", None),
    )
    out_specs = P("segment", None, "space", None, None, None)
    return jax.shard_map(body, mesh=mesh, in_specs=in_specs, out_specs=out_specs, check_vma=False)
```

```python
import functools

import jax
import jax.numpy as jnp
import numpy as np
from jax import lax
from jax.experimental import pallas as pl
from jax.experimental.pallas import tpu as pltpu
from jax.sharding import PartitionSpec as P

KS = 7
BPS = 2
EDGE = 1
MARGIN = KS // 2
PS = 8
CELLS = PS * PS
EXT = PS + 2 * MARGIN
WIDE = 3 * PS
TURNS = 4
MESH = pl.DeviceIdType.MESH
HOLDERS = {8: (2, 0, 1, 3, 5, 7, 6, 4)}

BIAS = 0
GAIN = 1
SCALE = 2
UP_BIAS = 3


def bases(neighbours, rotations, place, devices, tiles):
    count = neighbours.shape[0]
    local = neighbours - place * count
    following = lax.rem(place + 1, devices) * count
    slot = jnp.where(neighbours == following, count + 1, count)
    slot = jnp.where(jnp.logical_and(local >= 0, local < count), local, slot)
    slot = jnp.where(neighbours < 0, count + 2, slot)
    return (rotations * tiles + slot) * PS


def lookup(table, index):
    value = index
    for k, entry in enumerate(table):
        if entry != k:
            value = jnp.where(index == k, entry, value)
    return value


def position(space, devices):
    return lookup([HOLDERS.get(devices, range(devices)).index(k) for k in range(devices)], space)


def holder(place, devices):
    return lookup(HOLDERS.get(devices, range(devices)), place)


def gelu2(x):
    return x * (1.0 + lax.erf(x * np.float32(0.5**0.5)))


def kernel(
    segments,
    devices,
    blocks,
    field,
    taps,
    bias,
    gain,
    up,
    up_bias,
    down,
    scale,
    live_count,
    neighbours,
    rotations,
    out,
    v_taps,
    v_bias,
    v_gain,
    v_up_bias,
    v_scale,
    v_neighbours,
    v_rotations,
    meta,
    here,
    links,
    win,
    edges,
    ups,
    downs,
    small,
    tiles_a,
    tiles_b,
    ext,
    loc_sem,
    own_sem,
    w_recv,
    fwd_sem,
    h_send,
    h_recv,
    f_send,
    f_recv,
    o_send,
    o_recv,
    in_sem,
):
    space = lax.axis_index("space")
    me = lax.axis_index("segment")
    rows = win.shape[1]
    count = rows // CELLS
    tiles = count + 3
    place = position(space, devices)
    following = lax.rem(place + 1, devices)
    preceding = lax.rem(place + devices - 1, devices)
    after = holder(following, devices)
    before = holder(preceding, devices)
    core = lax.rem(me, 2)
    pair = me // 2
    partner = pair * 2 + (1 - core)
    pairs = segments // 2
    mine = me * BPS

    barrier = pltpu.get_barrier_semaphore()
    new_home = holder(space, devices)

    def greet(where, segment):
        other = jnp.logical_or(where != space, segment != me)

        @pl.when(other)
        def _():
            pl.semaphore_signal(
                barrier, inc=1, device_id=(where, segment), device_id_type=MESH
            )

        return jnp.where(other, 1, 0)

    greetings = 0
    for where in (before, after, preceding, place, following):
        greetings += greet(where, me)
    for step in range(1, segments):
        greetings += greet(space, lax.rem(me + step, segments))
    for segment in range(segments):
        greetings += greet(new_home, segment)

    own_up = pltpu.make_async_copy(up, ups.at[pl.ds(mine, BPS)], loc_sem.at[0])
    own_up.start()
    own_down = pltpu.make_async_copy(down, downs.at[pl.ds(mine, BPS)], loc_sem.at[1])
    own_down.start()
    loads = [
        pltpu.make_async_copy(src, dst, in_sem.at[n])
        for n, (src, dst) in enumerate(
            (
                (neighbours, v_neighbours),
                (rotations, v_rotations),
                (taps, v_taps),
                (bias, v_bias),
                (gain, v_gain),
                (up_bias, v_up_bias),
                (scale, v_scale),
            )
        )
    ]
    for load in loads:
        load.start()
    order = [count - 1, *range(count - 1)]
    half = 2 + (count - 2) // 2
    hid = up_bias.shape[1]
    chans = up.shape[1]
    for load in loads:
        load.wait()
    meta[...] = jnp.full(meta.shape, live_count[0], jnp.int32)
    meta[0:count, 0:8] = bases(v_neighbours[...], v_rotations[...], space, devices, tiles)
    for k in range(BPS):
        for row in range(KS):
            small[mine + k, row, 0:KS, :] = v_taps[
                row * KS : (row + 1) * KS, k, :
            ].astype(jnp.float32)
        small[mine + k, KS, BIAS : BIAS + 1, :] = v_bias[k : k + 1, :].astype(jnp.float32)
        small[mine + k, KS, GAIN : GAIN + 1, :] = v_gain[k : k + 1, :].astype(jnp.float32)
        small[mine + k, KS, SCALE : SCALE + 1, :] = 0.5 * jnp.exp2(
            v_scale[k : k + 1, :].astype(jnp.float32) * 0.5
        )
        for q in range(hid // chans):
            small[mine + k, KS, UP_BIAS + q : UP_BIAS + q + 1, :] = v_up_bias[
                k : k + 1, q * chans : (q + 1) * chans
            ].astype(jnp.float32)

    def flat(ref):
        return ref.reshape(ref.shape[0] * PS, chans)

    empty = jnp.zeros((CELLS, chans), jnp.float32)
    for turn in range(TURNS):
        at = (turn * tiles + count + 2) * CELLS
        flat(tiles_a)[at : at + CELLS, :] = empty
        flat(tiles_b)[at : at + CELLS, :] = empty
    pl.semaphore_wait(barrier, greetings)

    def send(src, dst, where, segment, send_sem, recv_sem):
        same = jnp.logical_and(where == space, segment == me)

        @pl.when(same)
        def _():
            pltpu.make_async_copy(src, dst, recv_sem).start()

        @pl.when(jnp.logical_not(same))
        def _():
            pltpu.make_async_remote_copy(
                src_ref=src,
                dst_ref=dst,
                send_sem=send_sem,
                recv_sem=recv_sem,
                device_id=(where, segment),
                device_id_type=MESH,
            ).start()

    def sent(src, dst, where, segment, send_sem, recv_sem):
        @pl.when(jnp.logical_not(jnp.logical_and(where == space, segment == me)))
        def _():
            pltpu.make_async_remote_copy(
                src_ref=src,
                dst_ref=dst,
                send_sem=send_sem,
                recv_sem=recv_sem,
                device_id=(where, segment),
                device_id_type=MESH,
            ).wait_send()

    def received(ref, recv_sem):
        pltpu.make_async_copy(ref, ref, recv_sem).wait()

    first = pl.ds(0, CELLS)
    last = pl.ds(rows - CELLS, CELLS)

    def lower(b):
        return edges.at[b, pl.ds(0, CELLS)]

    def upper(b):
        return edges.at[b, pl.ds(CELLS, CELLS)]

    ahead = holder(lax.rem(space + 1, devices), devices)
    behind = holder(lax.rem(space + devices - 1, devices), devices)
    moves = (
        (meta, here, new_home, me, f_send.at[0], f_recv.at[0]),
        (field.at[me, last], lower(0), ahead, me, f_send.at[1], h_recv.at[0, 0]),
        (field.at[me, first], upper(0), behind, me, f_send.at[2], h_recv.at[0, 1]),
        (field.at[me], win.at[0], new_home, me, f_send.at[3], f_recv.at[1]),
    )

    def halo(b, side):
        if side == 0:
            src, dst, to = win.at[b, last], lower(b), after
        else:
            src, dst, to = win.at[b, first], upper(b), before
        return pltpu.make_async_remote_copy(
            src_ref=src,
            dst_ref=dst,
            send_sem=h_send.at[b, side],
            recv_sem=h_recv.at[b, side],
            device_id=(to, me),
            device_id_type=MESH,
        )

    def piece(kind, b, to, send_sem):
        ref = (small, ups, downs)[kind].at[b]
        return pltpu.make_async_remote_copy(
            src_ref=ref,
            dst_ref=ref,
            send_sem=send_sem,
            recv_sem=w_recv.at[kind, b],
            device_id=(space, to),
            device_id_type=MESH,
        )

    def to_partner():
        return [
            piece(kind, mine + k, partner, own_sem.at[k, kind])
            for k in range(BPS)
            for kind in range(3)
        ]

    def to_pairs(k):
        copies = []
        for step in range(1, pairs):
            other = lax.rem(pair + step, pairs) * 2
            at = 3 + (step - 1) * 4
            copies.append(piece(0, mine + k, other, own_sem.at[k, at]))
            copies.append(piece(1, mine + k, other, own_sem.at[k, at + 2]))
            copies.append(piece(2, mine + k, other + 1, own_sem.at[k, at + 3]))
        return copies

    def turn_of(k):
        if k == 0:
            late = jnp.where(core == 0, 1, 4)
        else:
            late = jnp.where(core == 0, 2, 5)
        return jnp.where(pair == 0, -1, 2 * BPS * (pair - 1) + late)

    def forwarded(b, act):
        foreign = b // (2 * BPS) != pair

        @pl.when(jnp.logical_and(foreign, core == 0))
        def _():
            act(piece(0, b, partner, fwd_sem.at[1, b]))
            act(piece(1, b, partner, fwd_sem.at[0, b]))

        @pl.when(jnp.logical_and(foreign, core == 1))
        def _():
            act(piece(2, b, partner, fwd_sem.at[0, b]))

    def forward(b):
        def act(copy):
            copy.wait_recv()
            copy.start()

        forwarded(b, act)

    def arrive(b):
        owner = b // BPS
        foreign = b // (2 * BPS) != pair

        relayed = jnp.logical_and(foreign, core == 0)

        @pl.when(jnp.logical_and(owner != me, jnp.logical_not(relayed)))
        def _():
            piece(0, b, partner, fwd_sem.at[0, b]).wait_recv()

    def arrive_wide(b):
        owner = b // BPS
        foreign = b // (2 * BPS) != pair

        @pl.when(owner == partner)
        def _():
            piece(1, b, partner, fwd_sem.at[0, b]).wait_recv()
            piece(2, b, partner, fwd_sem.at[0, b]).wait_recv()

        @pl.when(jnp.logical_and(foreign, core == 0))
        def _():
            piece(2, b, partner, fwd_sem.at[0, b]).wait_recv()

        @pl.when(jnp.logical_and(foreign, core == 1))
        def _():
            piece(1, b, partner, fwd_sem.at[0, b]).wait_recv()

    chunks = ((count - 1, 1), (0, 1), (1, half - 2), (half - 1, count - half))

    def outcome(s, n):
        at = pl.ds(chunks[n][0] * CELLS, chunks[n][1] * CELLS)
        return (
            win.at[BPS * (s + 1), at],
            out.at[me, at],
            place,
            s,
            o_send.at[s, n],
            o_recv.at[me, n],
        )

    def spread(dst, slot, cells):
        dst = flat(dst)
        at = [(turn * tiles + slot) * CELLS for turn in range(TURNS)]
        for i in range(PS):
            row = cells[i * PS : (i + 1) * PS]
            dst[at[0] + i * PS : at[0] + (i + 1) * PS, :] = row
            dst[pl.ds(at[3] + PS - 1 - i, PS, stride=PS), :] = row
        for old, new in ((0, 1), (1, 2)):
            for j in range(PS):
                to = at[new] + (PS - 1 - j) * PS
                dst[to : to + PS, :] = dst[pl.ds(at[old] + j, PS, stride=PS), :]

    def middle(g):
        return (slice(g * EXT + MARGIN, g * EXT + MARGIN + PS), slice(PS, 2 * PS))

    def enter(dst, g, cells):
        spread(dst, g, cells)
        ext[middle(g)] = cells.reshape(PS, PS, chans)

    def margins(src, g):
        for d in range(8):
            band_i, band_j = ((0, 0), (0, 1), (0, 2), (1, 0), (1, 2), (2, 0), (2, 1), (2, 2))[d]
            base = links[g, d]
            if band_i == 0:
                lines = [(PS - MARGIN + i, i) for i in range(MARGIN)]
            elif band_i == 1:
                lines = [(i, MARGIN + i) for i in range(PS)]
            else:
                lines = [(i, MARGIN + PS + i) for i in range(MARGIN)]
            for i, to in lines:
                ext[g * EXT + to, band_j * PS : (band_j + 1) * PS, :] = src[base + i]

    def convolve(b, places):
        def line(a, total):
            for e in range(KS):
                window = jnp.concatenate(
                    [
                        ext[pl.ds(g * EXT + a, PS), PS - MARGIN + e : 2 * PS - MARGIN + e, :]
                        for g in places
                    ],
                    axis=0,
                )
                total = total + window * small[b, a, e : e + 1, :][None]
            return total

        start = small[b, KS, BIAS : BIAS + 1, :][None]
        start = jnp.broadcast_to(start, (len(places) * PS, PS, chans))
        total = lax.fori_loop(0, KS, line, start).reshape(-1, chans)
        centred = total - jnp.mean(total, axis=-1, keepdims=True)
        variance = jnp.mean(centred * centred, axis=-1, keepdims=True)
        scaled = centred * lax.rsqrt(variance + 1e-06) * small[b, KS, GAIN : GAIN + 1, :]
        return scaled.astype(jnp.bfloat16)

    def group(b, begin, end):
        normed = convolve(b, order[begin:end])
        if begin == 0:
            arrive_wide(b)
        wide = jnp.concatenate(
            [small[b, KS, UP_BIAS + q : UP_BIAS + q + 1, :] for q in range(hid // chans)], axis=1
        )
        hidden = jnp.dot(normed, ups[b], preferred_element_type=jnp.float32) + wide
        hidden = gelu2(hidden).astype(jnp.bfloat16)
        branch = jnp.dot(hidden, downs[b], preferred_element_type=jnp.float32)
        branch = branch * small[b, KS, SCALE : SCALE + 1, :]
        for n in range(begin, end):
            g = order[n]
            alive = jnp.logical_or(g < links[count, 0] - EDGE, g >= count - EDGE)
            alive = jnp.where(alive, 1.0, 0.0)
            old = ext[middle(g)].reshape(CELLS, chans)
            state = old + branch[(n - begin) * CELLS : (n - begin + 1) * CELLS]
            state = (state * alive).astype(jnp.bfloat16)
            win[b + 1, g * CELLS : (g + 1) * CELLS, :] = state

    def settle(b, begin, end, dst):
        for n in range(begin, end):
            g = order[n]
            enter(dst, g, win[b + 1, g * CELLS : (g + 1) * CELLS, :].astype(jnp.float32))

    for move in moves:
        send(*move)
    own_up.wait()
    own_down.wait()

    opening = me == 0

    @pl.when(opening)
    def _():
        for copy in to_pairs(0):
            copy.start()

    for copy in to_partner():
        copy.start()

    @pl.when(opening)
    def _():
        for copy in to_pairs(1):
            copy.start()

    forward(0)

    received(here, f_recv.at[0])
    table = pltpu.make_async_copy(here, links, loc_sem.at[2])
    table.start()
    received(win.at[0], f_recv.at[1])
    for g in range(count):
        enter(tiles_a, g, win[0, g * CELLS : (g + 1) * CELLS, :].astype(jnp.float32))
    table.wait()

    def layer(s, part):
        b = s * BPS + part
        src, dst = (tiles_a, tiles_b) if part % 2 == 0 else (tiles_b, tiles_a)
        arrive(b)
        for k in range(BPS):

            @pl.when(b == turn_of(k))
            def _():
                for copy in to_pairs(k):
                    copy.start()

        received(lower(b), h_recv.at[b, 0])
        received(upper(b), h_recv.at[b, 1])
        for side in range(2):
            tile = edges[b, side * CELLS : (side + 1) * CELLS, :].astype(jnp.float32)
            spread(src, count + side, tile)
        for n in range(2):
            margins(src, order[n])
        group(b, 0, 2)

        @pl.when(b < blocks - 1)
        def _():
            halo(b + 1, 0).start()
            halo(b + 1, 1).start()

        ends = part == BPS - 1
        if ends:
            send(*outcome(s, 0))
            send(*outcome(s, 1))
        settle(b, 0, 2, dst)
        for n in range(2, count):
            margins(src, order[n])
        group(b, 2, half)
        if ends:
            send(*outcome(s, 2))
        @pl.when(b < blocks - 1)
        def _():
            forward(b + 1)

        group(b, half, count)
        for k in range(BPS):

            @pl.when(jnp.logical_and(me == 1, b == k))
            def _():
                for copy in to_pairs(k):
                    copy.start()

        if ends:
            send(*outcome(s, 3))
        settle(b, 2, count, dst)

    def section(s, carry):
        for part in range(BPS):
            layer(s, part)
        return carry

    lax.fori_loop(0, segments, section, 0)

    for copy in to_partner() + to_pairs(0) + to_pairs(1):
        copy.wait_send()

    for move in moves:
        sent(*move)

    def drain(b, carry):
        @pl.when(b > 0)
        def _():
            halo(b, 0).wait_send()
            halo(b, 1).wait_send()

        forwarded(b, lambda copy: copy.wait_send())
        return carry

    lax.fori_loop(0, blocks, drain, 0)
    for s in range(segments):
        for n in range(len(chunks)):
            sent(*outcome(s, n))
    for member in range(segments):
        for n, (start, size) in enumerate(chunks):
            received(out.at[member, pl.ds(start * CELLS, size * CELLS)], o_recv.at[member, n])


def body(
    field,
    depth_kernel,
    depth_bias,
    norm_gain,
    up_weight,
    up_bias,
    down_weight,
    scale_exponent,
    live_count,
    neighbours,
    rotations,
):
    members, count = field.shape[:2]
    chans = field.shape[-1]
    hid = up_weight.shape[-1]
    segments = lax.axis_size("segment")
    devices = lax.axis_size("space")
    blocks = segments * BPS
    assert members == segments and segments % 2 == 0 and count % 2 == 0
    assert BPS == 2 and devices % 2 == 0
    pairs = segments // 2
    metas = count + 8
    assert UP_BIAS + hid // chans <= PS
    smem = pl.BlockSpec(memory_space=pltpu.SMEM)
    hbm = pl.BlockSpec(memory_space=pl.ANY)
    dma = pltpu.SemaphoreType.DMA
    out = pl.pallas_call(
        functools.partial(kernel, segments, devices, blocks),
        out_shape=pltpu.VMEM((members, count * CELLS, chans), jnp.bfloat16),
        in_specs=[hbm] * 8 + [smem] + [hbm] * 2,
        out_specs=pl.BlockSpec(memory_space=pltpu.VMEM),
        scratch_shapes=[
            pltpu.VMEM((KS * KS, BPS, chans), jnp.bfloat16),
            pltpu.VMEM((BPS, chans), jnp.bfloat16),
            pltpu.VMEM((BPS, chans), jnp.bfloat16),
            pltpu.VMEM((BPS, hid), jnp.bfloat16),
            pltpu.VMEM((BPS, chans), jnp.int32),
            pltpu.VMEM(neighbours.shape, jnp.int32),
            pltpu.VMEM(rotations.shape, jnp.int32),
            pltpu.VMEM((metas, chans), jnp.int32),
            pltpu.VMEM((metas, chans), jnp.int32),
            pltpu.SMEM((metas, chans), jnp.int32),
            pltpu.VMEM((blocks + 1, count * CELLS, chans), jnp.bfloat16),
            pltpu.VMEM((blocks, 2 * CELLS, chans), jnp.bfloat16),
            pltpu.VMEM((blocks, chans, hid), jnp.bfloat16),
            pltpu.VMEM((blocks, hid, chans), jnp.bfloat16),
            pltpu.VMEM((blocks, KS + 1, PS, chans), jnp.float32),
            pltpu.VMEM((TURNS * (count + 3) * PS, PS, chans), jnp.float32),
            pltpu.VMEM((TURNS * (count + 3) * PS, PS, chans), jnp.float32),
            pltpu.VMEM((count * EXT, WIDE, chans), jnp.float32),
            dma((3,)),
            dma((BPS, 3 + 4 * (pairs - 1))),
            dma((3, blocks)),
            dma((2, blocks)),
            dma((blocks, 2)),
            dma((blocks, 2)),
            dma((4,)),
            dma((2,)),
            dma((segments, 4)),
            dma((members, 4)),
            dma((7,)),
        ],
        compiler_params=pltpu.CompilerParams(
            collective_id=0, has_side_effects=True, vmem_limit_bytes=60 * 2**20
        ),
    )(
        field.reshape(members, count * CELLS, chans),
        jnp.transpose(depth_kernel, (1, 0, 2)),
        depth_bias,
        norm_gain,
        up_weight,
        up_bias,
        down_weight,
        scale_exponent,
        live_count,
        neighbours,
        rotations,
    )
    return out.reshape((1,) + field.shape)


def solution(mesh):
    in_specs = (
        P(None, "space", None, None, None),
        P("segment", None, None),
        P("segment", None),
        P("segment", None),
        P("segment", None, None),
        P("segment", None),
        P("segment", None, None),
        P("segment", None),
        P("space"),
        P("space", None),
        P("space", None),
    )
    out_specs = P("segment", None, "space", None, None, None)
    return jax.shard_map(body, mesh=mesh, in_specs=in_specs, out_specs=out_specs, check_vma=False)
```

```python
import functools

import jax
import jax.numpy as jnp
import numpy as np
from jax import lax
from jax.experimental import pallas as pl
from jax.experimental.pallas import tpu as pltpu
from jax.sharding import PartitionSpec as P

KS = 7
BPS = 2
EDGE = 1
MARGIN = KS // 2
PS = 8
CELLS = PS * PS
EXT = PS + 2 * MARGIN
WIDE = 3 * PS
TURNS = 4
MESH = pl.DeviceIdType.MESH
HOLDERS = {8: (2, 0, 1, 3, 5, 7, 6, 4)}

BIAS = 0
GAIN = 1
SCALE = 2
UP_BIAS = 3


def bases(neighbours, rotations, place, devices, tiles):
    count = neighbours.shape[0]
    local = neighbours - place * count
    following = lax.rem(place + 1, devices) * count
    slot = jnp.where(neighbours == following, count + 1, count)
    slot = jnp.where(jnp.logical_and(local >= 0, local < count), local, slot)
    slot = jnp.where(neighbours < 0, count + 2, slot)
    return (rotations * tiles + slot) * PS


def lookup(table, index):
    value = index
    for k, entry in enumerate(table):
        if entry != k:
            value = jnp.where(index == k, entry, value)
    return value


def position(space, devices):
    return lookup([HOLDERS.get(devices, range(devices)).index(k) for k in range(devices)], space)


def holder(place, devices):
    return lookup(HOLDERS.get(devices, range(devices)), place)


def gelu2(x):
    return x * (1.0 + lax.erf(x * np.float32(0.5**0.5)))


def kernel(
    segments,
    devices,
    blocks,
    field,
    taps,
    bias,
    gain,
    up,
    up_bias,
    down,
    scale,
    live_count,
    neighbours,
    rotations,
    out,
    v_taps,
    v_bias,
    v_gain,
    v_up_bias,
    v_scale,
    v_neighbours,
    v_rotations,
    meta,
    here,
    links,
    win,
    edges,
    ups,
    downs,
    small,
    tiles_a,
    tiles_b,
    ext,
    loc_sem,
    own_sem,
    w_recv,
    fwd_sem,
    h_send,
    h_recv,
    f_send,
    f_recv,
    o_send,
    o_recv,
    in_sem,
):
    space = lax.axis_index("space")
    me = lax.axis_index("segment")
    rows = win.shape[1]
    count = rows // CELLS
    tiles = count + 3
    place = position(space, devices)
    following = lax.rem(place + 1, devices)
    preceding = lax.rem(place + devices - 1, devices)
    after = holder(following, devices)
    before = holder(preceding, devices)
    core = lax.rem(me, 2)
    pair = me // 2
    partner = pair * 2 + (1 - core)
    pairs = segments // 2
    mine = me * BPS

    barrier = pltpu.get_barrier_semaphore()
    new_home = holder(space, devices)

    def greet(where, segment):
        other = jnp.logical_or(where != space, segment != me)

        @pl.when(other)
        def _():
            pl.semaphore_signal(
                barrier, inc=1, device_id=(where, segment), device_id_type=MESH
            )

        return jnp.where(other, 1, 0)

    greetings = 0
    for where in (before, after, preceding, place, following):
        greetings += greet(where, me)
    for step in range(1, segments):
        greetings += greet(space, lax.rem(me + step, segments))
    for segment in range(segments):
        greetings += greet(new_home, segment)

    own_up = pltpu.make_async_copy(up, ups.at[pl.ds(mine, BPS)], loc_sem.at[0])
    own_up.start()
    own_down = pltpu.make_async_copy(down, downs.at[pl.ds(mine, BPS)], loc_sem.at[1])
    own_down.start()
    loads = [
        pltpu.make_async_copy(src, dst, in_sem.at[n])
        for n, (src, dst) in enumerate(
            (
                (neighbours, v_neighbours),
                (rotations, v_rotations),
                (taps, v_taps),
                (bias, v_bias),
                (gain, v_gain),
                (up_bias, v_up_bias),
                (scale, v_scale),
            )
        )
    ]
    for load in loads:
        load.start()
    order = [count - 1, *range(count - 1)]
    half = 2 + (count - 2) // 2
    hid = up_bias.shape[1]
    chans = up.shape[1]
    for load in loads:
        load.wait()
    meta[...] = jnp.full(meta.shape, live_count[0], jnp.int32)
    meta[0:count, 0:8] = bases(v_neighbours[...], v_rotations[...], space, devices, tiles)
    for k in range(BPS):
        for row in range(KS):
            small[mine + k, row, 0:KS, :] = v_taps[
                row * KS : (row + 1) * KS, k, :
            ].astype(jnp.float32)
        small[mine + k, KS, BIAS : BIAS + 1, :] = v_bias[k : k + 1, :].astype(jnp.float32)
        small[mine + k, KS, GAIN : GAIN + 1, :] = v_gain[k : k + 1, :].astype(jnp.float32)
        small[mine + k, KS, SCALE : SCALE + 1, :] = 0.5 * jnp.exp2(
            v_scale[k : k + 1, :].astype(jnp.float32) * 0.5
        )
        for q in range(hid // chans):
            small[mine + k, KS, UP_BIAS + q : UP_BIAS + q + 1, :] = v_up_bias[
                k : k + 1, q * chans : (q + 1) * chans
            ].astype(jnp.float32)

    def flat(ref):
        return ref.reshape(ref.shape[0] * PS, chans)

    empty = jnp.zeros((CELLS, chans), jnp.float32)
    for turn in range(TURNS):
        at = (turn * tiles + count + 2) * CELLS
        flat(tiles_a)[at : at + CELLS, :] = empty
        flat(tiles_b)[at : at + CELLS, :] = empty
    pl.semaphore_wait(barrier, greetings)

    def send(src, dst, where, segment, send_sem, recv_sem):
        same = jnp.logical_and(where == space, segment == me)

        @pl.when(same)
        def _():
            pltpu.make_async_copy(src, dst, recv_sem).start()

        @pl.when(jnp.logical_not(same))
        def _():
            pltpu.make_async_remote_copy(
                src_ref=src,
                dst_ref=dst,
                send_sem=send_sem,
                recv_sem=recv_sem,
                device_id=(where, segment),
                device_id_type=MESH,
            ).start()

    def sent(src, dst, where, segment, send_sem, recv_sem):
        @pl.when(jnp.logical_not(jnp.logical_and(where == space, segment == me)))
        def _():
            pltpu.make_async_remote_copy(
                src_ref=src,
                dst_ref=dst,
                send_sem=send_sem,
                recv_sem=recv_sem,
                device_id=(where, segment),
                device_id_type=MESH,
            ).wait_send()

    def received(ref, recv_sem):
        pltpu.make_async_copy(ref, ref, recv_sem).wait()

    first = pl.ds(0, CELLS)
    last = pl.ds(rows - CELLS, CELLS)

    def lower(b):
        return edges.at[b, pl.ds(0, CELLS)]

    def upper(b):
        return edges.at[b, pl.ds(CELLS, CELLS)]

    ahead = holder(lax.rem(space + 1, devices), devices)
    behind = holder(lax.rem(space + devices - 1, devices), devices)
    moves = (
        (meta, here, new_home, me, f_send.at[0], f_recv.at[0]),
        (field.at[me, last], lower(0), ahead, me, f_send.at[1], h_recv.at[0, 0]),
        (field.at[me, first], upper(0), behind, me, f_send.at[2], h_recv.at[0, 1]),
        (field.at[me], win.at[0], new_home, me, f_send.at[3], f_recv.at[1]),
    )

    def halo(b, side):
        if side == 0:
            src, dst, to = win.at[b, last], lower(b), after
        else:
            src, dst, to = win.at[b, first], upper(b), before
        return pltpu.make_async_remote_copy(
            src_ref=src,
            dst_ref=dst,
            send_sem=h_send.at[b, side],
            recv_sem=h_recv.at[b, side],
            device_id=(to, me),
            device_id_type=MESH,
        )

    def piece(kind, b, to, send_sem):
        ref = (small, ups, downs)[kind].at[b]
        return pltpu.make_async_remote_copy(
            src_ref=ref,
            dst_ref=ref,
            send_sem=send_sem,
            recv_sem=w_recv.at[kind, b],
            device_id=(space, to),
            device_id_type=MESH,
        )

    def to_partner():
        return [
            piece(kind, mine + k, partner, own_sem.at[k, kind])
            for k in range(BPS)
            for kind in range(3)
        ]

    def to_pairs(k):
        copies = []
        for step in range(1, pairs):
            other = lax.rem(pair + step, pairs) * 2
            at = 3 + (step - 1) * 4
            copies.append(piece(0, mine + k, other, own_sem.at[k, at]))
            copies.append(piece(1, mine + k, other, own_sem.at[k, at + 2]))
            copies.append(piece(2, mine + k, other + 1, own_sem.at[k, at + 3]))
        return copies

    def turn_of(k):
        if k == 0:
            late = jnp.where(core == 0, 1, 4)
        else:
            late = jnp.where(core == 0, 2, 5)
        return jnp.where(pair == 0, -1, 2 * BPS * (pair - 1) + late)

    def forwarded(b, act):
        foreign = b // (2 * BPS) != pair

        @pl.when(jnp.logical_and(foreign, core == 0))
        def _():
            act(piece(0, b, partner, fwd_sem.at[1, b]))
            act(piece(1, b, partner, fwd_sem.at[0, b]))

        @pl.when(jnp.logical_and(foreign, core == 1))
        def _():
            act(piece(2, b, partner, fwd_sem.at[0, b]))

    def forward(b):
        def act(copy):
            copy.wait_recv()
            copy.start()

        forwarded(b, act)

    def arrive(b):
        owner = b // BPS
        foreign = b // (2 * BPS) != pair

        relayed = jnp.logical_and(foreign, core == 0)

        @pl.when(jnp.logical_and(owner != me, jnp.logical_not(relayed)))
        def _():
            piece(0, b, partner, fwd_sem.at[0, b]).wait_recv()

    def arrive_wide(b):
        owner = b // BPS
        foreign = b // (2 * BPS) != pair

        @pl.when(owner == partner)
        def _():
            piece(1, b, partner, fwd_sem.at[0, b]).wait_recv()
            piece(2, b, partner, fwd_sem.at[0, b]).wait_recv()

        @pl.when(jnp.logical_and(foreign, core == 0))
        def _():
            piece(2, b, partner, fwd_sem.at[0, b]).wait_recv()

        @pl.when(jnp.logical_and(foreign, core == 1))
        def _():
            piece(1, b, partner, fwd_sem.at[0, b]).wait_recv()

    chunks = ((count - 1, 1), (0, 1), (1, half - 2), (half - 1, count - half))

    def outcome(s, n):
        at = pl.ds(chunks[n][0] * CELLS, chunks[n][1] * CELLS)
        return (
            win.at[BPS * (s + 1), at],
            out.at[me, at],
            place,
            s,
            o_send.at[s, n],
            o_recv.at[me, n],
        )

    def spread(dst, slot, cells):
        dst = flat(dst)
        at = [(turn * tiles + slot) * CELLS for turn in range(TURNS)]
        for i in range(PS):
            row = cells[i * PS : (i + 1) * PS]
            dst[at[0] + i * PS : at[0] + (i + 1) * PS, :] = row
            dst[pl.ds(at[3] + PS - 1 - i, PS, stride=PS), :] = row
        for old, new in ((0, 1), (1, 2)):
            for j in range(PS):
                to = at[new] + (PS - 1 - j) * PS
                dst[to : to + PS, :] = dst[pl.ds(at[old] + j, PS, stride=PS), :]

    def middle(g):
        return (slice(g * EXT + MARGIN, g * EXT + MARGIN + PS), slice(PS, 2 * PS))

    def enter(dst, g, cells):
        spread(dst, g, cells)
        ext[middle(g)] = cells.reshape(PS, PS, chans)

    def margins(src, g):
        for d in range(8):
            band_i, band_j = ((0, 0), (0, 1), (0, 2), (1, 0), (1, 2), (2, 0), (2, 1), (2, 2))[d]
            base = links[g, d]
            if band_i == 0:
                lines = [(PS - MARGIN + i, i) for i in range(MARGIN)]
            elif band_i == 1:
                lines = [(i, MARGIN + i) for i in range(PS)]
            else:
                lines = [(i, MARGIN + PS + i) for i in range(MARGIN)]
            for i, to in lines:
                ext[g * EXT + to, band_j * PS : (band_j + 1) * PS, :] = src[base + i]

    def convolve(b, places):
        def line(a, total):
            for e in range(KS):
                window = jnp.concatenate(
                    [
                        ext[pl.ds(g * EXT + a, PS), PS - MARGIN + e : 2 * PS - MARGIN + e, :]
                        for g in places
                    ],
                    axis=0,
                )
                total = total + window * small[b, a, e : e + 1, :][None]
            return total

        start = small[b, KS, BIAS : BIAS + 1, :][None]
        start = jnp.broadcast_to(start, (len(places) * PS, PS, chans))
        total = lax.fori_loop(0, KS, line, start).reshape(-1, chans)
        centred = total - jnp.mean(total, axis=-1, keepdims=True)
        variance = jnp.mean(centred * centred, axis=-1, keepdims=True)
        scaled = centred * lax.rsqrt(variance + 1e-06) * small[b, KS, GAIN : GAIN + 1, :]
        return scaled.astype(jnp.bfloat16)

    def group(b, begin, end):
        normed = convolve(b, order[begin:end])
        if begin == 0:
            arrive_wide(b)
        wide = jnp.concatenate(
            [small[b, KS, UP_BIAS + q : UP_BIAS + q + 1, :] for q in range(hid // chans)], axis=1
        )
        hidden = jnp.dot(normed, ups[b], preferred_element_type=jnp.float32) + wide
        hidden = gelu2(hidden).astype(jnp.bfloat16)
        branch = jnp.dot(hidden, downs[b], preferred_element_type=jnp.float32)
        branch = branch * small[b, KS, SCALE : SCALE + 1, :]
        for n in range(begin, end):
            g = order[n]
            alive = jnp.logical_or(g < links[count, 0] - EDGE, g >= count - EDGE)
            alive = jnp.where(alive, 1.0, 0.0)
            old = ext[middle(g)].reshape(CELLS, chans)
            state = old + branch[(n - begin) * CELLS : (n - begin + 1) * CELLS]
            state = (state * alive).astype(jnp.bfloat16)
            win[b + 1, g * CELLS : (g + 1) * CELLS, :] = state

    def settle(b, begin, end, dst):
        for n in range(begin, end):
            g = order[n]
            enter(dst, g, win[b + 1, g * CELLS : (g + 1) * CELLS, :].astype(jnp.float32))

    for move in moves[:3]:
        send(*move)
    own_up.wait()
    own_down.wait()

    opening = me == 0

    @pl.when(opening)
    def _():
        for copy in to_pairs(0):
            copy.start()

    send(*moves[3])
    for copy in to_partner():
        copy.start()

    @pl.when(opening)
    def _():
        for copy in to_pairs(1):
            copy.start()

    forward(0)

    received(here, f_recv.at[0])
    table = pltpu.make_async_copy(here, links, loc_sem.at[2])
    table.start()
    received(win.at[0], f_recv.at[1])
    for g in range(count):
        enter(tiles_a, g, win[0, g * CELLS : (g + 1) * CELLS, :].astype(jnp.float32))
    table.wait()

    def layer(s, part):
        b = s * BPS + part
        src, dst = (tiles_a, tiles_b) if part % 2 == 0 else (tiles_b, tiles_a)
        arrive(b)
        for k in range(BPS):

            @pl.when(b == turn_of(k))
            def _():
                for copy in to_pairs(k):
                    copy.start()

        received(lower(b), h_recv.at[b, 0])
        received(upper(b), h_recv.at[b, 1])
        for side in range(2):
            tile = edges[b, side * CELLS : (side + 1) * CELLS, :].astype(jnp.float32)
            spread(src, count + side, tile)
        for n in range(2):
            margins(src, order[n])
        group(b, 0, 2)

        @pl.when(b < blocks - 1)
        def _():
            halo(b + 1, 0).start()
            halo(b + 1, 1).start()

        ends = part == BPS - 1
        if ends:
            send(*outcome(s, 0))
            send(*outcome(s, 1))
        settle(b, 0, 2, dst)
        for n in range(2, count):
            margins(src, order[n])
        group(b, 2, half)
        if ends:
            send(*outcome(s, 2))
        @pl.when(b < blocks - 1)
        def _():
            forward(b + 1)

        group(b, half, count)
        for k in range(BPS):

            @pl.when(jnp.logical_and(me == 1, b == k))
            def _():
                for copy in to_pairs(k):
                    copy.start()

        if ends:
            send(*outcome(s, 3))
        settle(b, 2, count, dst)

    def section(s, carry):
        for part in range(BPS):
            layer(s, part)
        return carry

    lax.fori_loop(0, segments, section, 0)

    for copy in to_partner() + to_pairs(0) + to_pairs(1):
        copy.wait_send()

    for move in moves:
        sent(*move)

    def drain(b, carry):
        @pl.when(b > 0)
        def _():
            halo(b, 0).wait_send()
            halo(b, 1).wait_send()

        forwarded(b, lambda copy: copy.wait_send())
        return carry

    lax.fori_loop(0, blocks, drain, 0)
    for s in range(segments):
        for n in range(len(chunks)):
            sent(*outcome(s, n))
    for member in range(segments):
        for n, (start, size) in enumerate(chunks):
            received(out.at[member, pl.ds(start * CELLS, size * CELLS)], o_recv.at[member, n])


def body(
    field,
    depth_kernel,
    depth_bias,
    norm_gain,
    up_weight,
    up_bias,
    down_weight,
    scale_exponent,
    live_count,
    neighbours,
    rotations,
):
    members, count = field.shape[:2]
    chans = field.shape[-1]
    hid = up_weight.shape[-1]
    segments = lax.axis_size("segment")
    devices = lax.axis_size("space")
    blocks = segments * BPS
    assert members == segments and segments % 2 == 0 and count % 2 == 0
    assert BPS == 2 and devices % 2 == 0
    pairs = segments // 2
    metas = count + 8
    assert UP_BIAS + hid // chans <= PS
    smem = pl.BlockSpec(memory_space=pltpu.SMEM)
    hbm = pl.BlockSpec(memory_space=pl.ANY)
    dma = pltpu.SemaphoreType.DMA
    out = pl.pallas_call(
        functools.partial(kernel, segments, devices, blocks),
        out_shape=pltpu.VMEM((members, count * CELLS, chans), jnp.bfloat16),
        in_specs=[hbm] * 8 + [smem] + [hbm] * 2,
        out_specs=pl.BlockSpec(memory_space=pltpu.VMEM),
        scratch_shapes=[
            pltpu.VMEM((KS * KS, BPS, chans), jnp.bfloat16),
            pltpu.VMEM((BPS, chans), jnp.bfloat16),
            pltpu.VMEM((BPS, chans), jnp.bfloat16),
            pltpu.VMEM((BPS, hid), jnp.bfloat16),
            pltpu.VMEM((BPS, chans), jnp.int32),
            pltpu.VMEM(neighbours.shape, jnp.int32),
            pltpu.VMEM(rotations.shape, jnp.int32),
            pltpu.VMEM((metas, chans), jnp.int32),
            pltpu.VMEM((metas, chans), jnp.int32),
            pltpu.SMEM((metas, chans), jnp.int32),
            pltpu.VMEM((blocks + 1, count * CELLS, chans), jnp.bfloat16),
            pltpu.VMEM((blocks, 2 * CELLS, chans), jnp.bfloat16),
            pltpu.VMEM((blocks, chans, hid), jnp.bfloat16),
            pltpu.VMEM((blocks, hid, chans), jnp.bfloat16),
            pltpu.VMEM((blocks, KS + 1, PS, chans), jnp.float32),
            pltpu.VMEM((TURNS * (count + 3) * PS, PS, chans), jnp.float32),
            pltpu.VMEM((TURNS * (count + 3) * PS, PS, chans), jnp.float32),
            pltpu.VMEM((count * EXT, WIDE, chans), jnp.float32),
            dma((3,)),
            dma((BPS, 3 + 4 * (pairs - 1))),
            dma((3, blocks)),
            dma((2, blocks)),
            dma((blocks, 2)),
            dma((blocks, 2)),
            dma((4,)),
            dma((2,)),
            dma((segments, 4)),
            dma((members, 4)),
            dma((7,)),
        ],
        compiler_params=pltpu.CompilerParams(
            collective_id=0, has_side_effects=True, vmem_limit_bytes=60 * 2**20
        ),
    )(
        field.reshape(members, count * CELLS, chans),
        jnp.transpose(depth_kernel, (1, 0, 2)),
        depth_bias,
        norm_gain,
        up_weight,
        up_bias,
        down_weight,
        scale_exponent,
        live_count,
        neighbours,
        rotations,
    )
    return out.reshape((1,) + field.shape)


def solution(mesh):
    in_specs = (
        P(None, "space", None, None, None),
        P("segment", None, None),
        P("segment", None),
        P("segment", None),
        P("segment", None, None),
        P("segment", None),
        P("segment", None, None),
        P("segment", None),
        P("space"),
        P("space", None),
        P("space", None),
    )
    out_specs = P("segment", None, "space", None, None, None)
    return jax.shard_map(body, mesh=mesh, in_specs=in_specs, out_specs=out_specs, check_vma=False)
```
